32 devices in a mesh: seastate: 2 (over y), bx: 4 (over z), by: 4 (over x, core).
Axes of the slice: x: 2, y: 2, z: 4, core: 2. Of those that a mesh axis runs over, the one named last changes fastest.
Arguments:
- leaf_factor: bfloat16 [4, 4, 128, 128, 128], P('bx', 'by', 'seastate'), parts along dimension 2, may hold values from -0.5 to 0.5
- class_maps: bfloat16 [16, 128, 128], P('seastate'), parts along dimension 0, may hold values from -1.25 to 1.25
- depth_class: int32 [4, 4, 128], P('bx', None, 'seastate'), parts along dimension 2, may hold values from 0 to 7
- owners: int32 [4, 4, 128, 1], P('bx', 'by', 'seastate'), parts along dimension 2, may hold values from 0 to 3; in each aligned block of 64 rows (0 to 63, 64 to 127, ..., all dimensions but the last counted through in order) at most 24 rows name the same one
- top_in: float32 [4, 4, 32, 256], P('bx', 'by', 'seastate'), parts along dimension 2, may hold values from -6 to 6
Outputs:
- top_out: float32 [4, 4, 32, 256], P('bx', 'by', 'seastate'), parts along dimension 2
- delivered: float32 [4, 4, 4, 48, 128], P('bx', 'by', None, 'seastate'), parts along dimension 3
The draws below stay inside these ranges and needn't reach their ends.
There are 2 independent parts, one for each index of `seastate`. The reference program is written for one: setup_inputs(seed, part) draws one part's arguments, and reference() takes and returns one part's arrays. A program takes and returns all parts, laid end to end along the dimension named above; each array names one. Nothing has to cross between parts.
Inputs may be any that keep to these rules, and one draw needn't show every extreme that they name: `owners`: among the 64 leaves of one device no bx index is named more than 24 times.
All inputs are finite; a program needn't handle non-finite values.
Results may differ from the reference program's by a relative error of at most 0.0003.
Values may be sent and summed in bfloat16 or wider, within the bound.
A program may use at most 128 MiB of HBM per device.

```python
import math
import jax
import jax.numpy as jnp
import numpy as np
from jax import lax

FACE = 32
LEAF = 128
CLASSES = 8
NB = 64
MOST = 24
N_BX = 4
N_BY = 4


def touch_ends(values, rng, least, high):
    place = [jax.random.randint(jax.random.fold_in(rng, axis), (), 0, length) for axis, length in enumerate(values.shape)]
    widest = values.shape.index(max(values.shape))
    next_to = place[:widest] + [(place[widest] + 1) % values.shape[widest]] + place[widest + 1:]
    return values.at[tuple(place)].set(least).at[tuple(next_to)].set(high)


def block_scale(rng, dims, cuts, least, high):
    factor_of = 1.0
    for axis_at, shards_of in cuts:
        draws = jax.random.uniform(jax.random.fold_in(jax.random.fold_in(rng, 6), axis_at), (shards_of,), jnp.float32, least / len(cuts), high / len(cuts))
        factor_of = factor_of * jnp.repeat(jnp.exp(draws), dims[axis_at] // shards_of).reshape((-1,) + (1,) * (len(dims) - 1 - axis_at))
    return factor_of


def routed_block(stream_key, own, number, rows, number_of, top, bound, skew):
    sequence = jax.random.permutation(stream_key, number_of)
    packed, common = portions_of(number_of, rows * top, bound, skew, True), portions_of(number_of, rows * top, bound, skew, False)
    places = jnp.arange(number_of)

    def named(sizes, rotation):
        used = int((sizes > 0).sum())
        fixed = max(1, used // 4)
        moved = fixed + (places - fixed + rotation * (used - fixed)) % max(1, number_of - fixed)
        return jnp.zeros((number_of,), jnp.int32).at[sequence[jnp.where(places < fixed, places, moved)]].set(jnp.asarray(sizes, jnp.int32))

    sizes = jnp.where(number % 4 == 0, named(packed, number // 4), named(common, number - number // 4 - 1))
    mixed = jax.random.permutation(jax.random.fold_in(own, 3), number_of)
    source_of, sink = mixed[0:number_of // 2 * 2:2], mixed[1:number_of // 2 * 2:2]
    room = jnp.minimum(sizes[source_of] - 1, bound - sizes[sink]) // 2
    room = jnp.where((source_of == sequence[0]) | (sink == sequence[0]) | (sizes[sink] == 0), 0, jnp.maximum(room, 0))
    moved = jax.random.randint(jax.random.fold_in(own, 4), (number_of // 2,), 0, 1 << 20) % (room + 1)
    sizes = sizes.at[source_of].add(-moved).at[sink].add(moved)
    members = jnp.searchsorted(jnp.cumsum(sizes), jnp.arange(rows * top), side="right").astype(jnp.int32)
    listing = members.reshape(top, rows).T
    listing = listing[jax.random.permutation(jax.random.fold_in(own, 1), rows)]
    rotation = jax.random.randint(jax.random.fold_in(own, 2), (rows, 1), 0, top)
    return jnp.take_along_axis(listing, (jnp.arange(top)[None, :] + rotation) % top, axis=1)


def portions_of(amount, total, reach, skew, full):
    weights = [(1 << 20) // math.isqrt(rank ** skew) + 1 for rank in range(1, amount + 1)]
    largest = reach if full else min(reach, max(-(-total // amount), total * weights[0] // sum(weights)))
    least = 1 if total - largest >= amount - 1 else 0
    given, rest = [largest] + [least] * (amount - 1), total - largest - least * (amount - 1)
    while rest > 0:
        movable = [i for i in range(1, amount) if given[i] < largest] or [i for i in range(1, amount) if given[i] < reach]
        mass, remaining = sum([weights[i] for i in movable]), rest
        for i in movable:
            addition = min(reach - given[i], max(1, remaining * weights[i] // mass), rest)
            given[i] = given[i] + addition
            rest = rest - addition
    return np.array(given)


def noise(stream_key, shape, width, bound, cuts=(), held_as=jnp.bfloat16):
    result = jax.random.normal(stream_key, shape, jnp.float32) * width
    if len(cuts) > 0:
        result = block_scale(stream_key, shape, cuts, -0.22, 0.18) * result
    return jnp.clip(result, min=-bound, max=bound).astype(held_as)


def setup_inputs(seed: int = 0, part: int = 0) -> dict:
    streams_of = jax.random.split(jax.random.key(seed), 6)
    own_keys = jax.random.split(jax.random.fold_in(streams_of[5], part), 6)
    leaf_factor = noise(own_keys[0], (N_BX, N_BY, NB, LEAF, LEAF), LEAF ** -0.5, 0.5, ((0, 4), (1, 4)))
    class_maps = noise(own_keys[1], (CLASSES, LEAF, LEAF), 0.09, 1.25)
    depth_class = touch_ends(jax.random.randint(own_keys[2], (N_BX, N_BY, NB), 0, CLASSES), jax.random.fold_in(own_keys[2], 1), 0, CLASSES - 1).astype(jnp.int32)
    owners_keys = jax.random.split(jax.random.fold_in(own_keys[3], 1), N_BX * N_BY * NB // NB)
    owners_turns = jax.random.permutation(jax.random.fold_in(own_keys[3], 3), N_BX * N_BY * NB // NB)
    owners = jax.vmap(lambda own, number: routed_block(jax.random.fold_in(own_keys[3], 2), own, number, NB, N_BX, 1, MOST, 2))(owners_keys, owners_turns).reshape((N_BX, N_BY, NB, 1))
    top_in = noise(own_keys[4], (N_BX, N_BY, NB // 4, 8 * FACE), 1.0, 6.0, ((0, 4), (1, 4)), jnp.float32)
    return {"leaf_factor": leaf_factor, "class_maps": class_maps, "depth_class": depth_class, "owners": owners, "top_in": top_in}


def take_ranges(matrix, ranges, axis):
    parts = [lax.slice_in_dim(matrix, begin, finish, axis=axis) for begin, finish in ranges]
    if len(parts) == 1:
        return parts[0]
    return jnp.concatenate(parts, axis=axis)


def low_tables(face):
    return ([(0, 3 * face)], [(3 * face, 4 * face)], [(0, 2 * face), (3 * face, 4 * face)], [(2 * face, 3 * face)],
            [(0, face), (3 * face, 4 * face), (face, 2 * face), (4 * face, 5 * face), (2 * face, 3 * face), (5 * face, 6 * face)],
            [(0, face), (2 * face, 3 * face), (4 * face, 5 * face), (face, 2 * face), (3 * face, 4 * face), (5 * face, 6 * face)])


def high_tables(face):
    return ([(0, 2 * face), (4 * face, 6 * face)], [(2 * face, 4 * face)], [(2 * face, 6 * face)], [(0, 2 * face)],
            [(0, 2 * face), (4 * face, 6 * face), (2 * face, 3 * face), (6 * face, 7 * face), (3 * face, 4 * face), (7 * face, 8 * face)],
            [(0, 2 * face), (4 * face, 5 * face), (6 * face, 7 * face), (2 * face, 4 * face), (5 * face, 6 * face), (7 * face, 8 * face)])


def product(left, right):
    return jnp.einsum('nij,njk->nik', left, right, precision=lax.Precision.HIGHEST)


def apply_map(matrix, vector):
    return jnp.einsum('nij,nj->ni', matrix, vector, precision=lax.Precision.HIGHEST)


def block_of(matrix, rows, columns):
    return take_ranges(take_ranges(matrix, rows, 1), columns, 2)


def merge_boxes(map_a, map_b, tables):
    ext_a, int_a, ext_b, int_b, order, back = tables
    a_ee = block_of(map_a, ext_a, ext_a)
    a_es = block_of(map_a, ext_a, int_a)
    a_se = block_of(map_a, int_a, ext_a)
    a_ss = block_of(map_a, int_a, int_a)
    b_ee = block_of(map_b, ext_b, ext_b)
    b_es = block_of(map_b, ext_b, int_b)
    b_se = block_of(map_b, int_b, ext_b)
    b_ss = block_of(map_b, int_b, int_b)
    count = a_ss.shape[0]
    inner = a_ss.shape[1]
    width_a = a_ee.shape[1]
    width_b = b_ee.shape[1]
    identity = jnp.eye(inner, dtype=jnp.float32)
    crossed = product(b_ss, a_ss)
    inverse = identity + product(crossed, identity + product(crossed, identity + crossed))
    inward_a = product(inverse, jnp.concatenate([product(b_ss, a_se), -b_se], axis=2))
    inward_b = -jnp.concatenate([a_se, jnp.zeros((count, inner, width_b), jnp.float32)], axis=2) - product(a_ss, inward_a)
    upper_rows = jnp.concatenate([a_ee, jnp.zeros((count, width_a, width_b), jnp.float32)], axis=2) + product(a_es, inward_a)
    lower_rows = jnp.concatenate([jnp.zeros((count, width_b, width_a), jnp.float32), b_ee], axis=2) + product(b_es, inward_b)
    merged = block_of(jnp.concatenate([upper_rows, lower_rows], axis=1), order, order)
    return merged, inward_a, inward_b


def descend_high(fields, inward_a, inward_b, back, face):
    joined = take_ranges(fields, back, 1)
    part_a = apply_map(inward_a, joined)
    part_b = apply_map(inward_b, joined)
    west = jnp.concatenate([joined[:, :2 * face], part_a, joined[:, 2 * face:4 * face]], axis=1)
    east = jnp.concatenate([part_b, joined[:, 4 * face:]], axis=1)
    return west, east


def descend_low(fields, inward_a, inward_b, back, face):
    joined = take_ranges(fields, back, 1)
    part_a = apply_map(inward_a, joined)
    part_b = apply_map(inward_b, joined)
    south = jnp.concatenate([joined[:, :3 * face], part_a], axis=1)
    north = jnp.concatenate([joined[:, 3 * face:5 * face], part_b, joined[:, 5 * face:6 * face]], axis=1)
    return south, north


def reference(leaf_factor, class_maps, depth_class, owners, top_in):
    face = FACE
    quarter = NB // 4
    low = low_tables(face)
    high = high_tables(face)
    pairs_y = N_BY // 2
    pairs_x = N_BX // 2

    def quad(index):
        column = (index // pairs_y).astype(jnp.int32)
        row = (index % pairs_y).astype(jnp.int32)
        zero = jnp.zeros((), jnp.int32)
        start_x = (2 * column).astype(jnp.int32)
        start_y = (2 * row).astype(jnp.int32)
        factor = lax.dynamic_slice(leaf_factor, (start_x, start_y, zero, zero, zero), (2, 2, NB, LEAF, LEAF))
        classes = lax.dynamic_slice(depth_class, (start_x, start_y, zero), (2, 2, NB))
        incoming = lax.dynamic_slice(top_in, (start_x, start_y, zero, zero), (2, 2, quarter, 8 * face))
        onehot = (classes[..., None] == jnp.arange(CLASSES, dtype=jnp.int32)).astype(jnp.float32)
        chosen = jnp.einsum('ijkc,cab->ijkab', onehot, class_maps.astype(jnp.float32))
        maps = jnp.einsum('ijkab,ijkbc->ijkac', chosen, factor.astype(jnp.float32))
        level_one, cross_one, back_one = merge_boxes(maps[:, 0].reshape(2 * NB, LEAF, LEAF),
                                                     maps[:, 1].reshape(2 * NB, LEAF, LEAF), low)
        top_map, cross_two, back_two = merge_boxes(level_one[:NB], level_one[NB:], high)
        fields = incoming.transpose(1, 0, 2, 3).reshape(NB, 8 * face)
        outgoing = apply_map(top_map, fields).reshape(2, 2, quarter, 8 * face).transpose(1, 0, 2, 3)
        west, east = descend_high(fields, cross_two, back_two, high[5], face)
        lower_fields = jnp.concatenate([west, east], axis=0)
        south, north = descend_low(lower_fields, cross_one, back_one, low[5], face)
        leaves = jnp.stack([south.reshape(2, NB, LEAF), north.reshape(2, NB, LEAF)], axis=1)
        return outgoing, leaves

    outs, leaves = lax.map(quad, jnp.arange(pairs_x * pairs_y, dtype=jnp.int32))
    outs = outs.reshape(pairs_x, pairs_y, 2, 2, quarter, 8 * face).transpose(0, 2, 1, 3, 4, 5)
    top_out = outs.reshape(N_BX, N_BY, quarter, 8 * face)
    leaves = leaves.reshape(pairs_x, pairs_y, 2, 2, NB, LEAF).transpose(0, 2, 1, 3, 4, 5).reshape(N_BX, N_BY, NB, LEAF)
    target = owners[..., 0].astype(jnp.int32)
    onehot = (target[..., None] == jnp.arange(N_BX, dtype=jnp.int32)).astype(jnp.int32)
    rank = jnp.sum((jnp.cumsum(onehot, axis=2) - onehot) * onehot, axis=3).astype(jnp.int32)
    home_ids = jnp.broadcast_to(jnp.arange(N_BX, dtype=jnp.int32)[:, None, None], target.shape)
    row_ids = jnp.broadcast_to(jnp.arange(N_BY, dtype=jnp.int32)[None, :, None], target.shape)
    delivered = jnp.zeros((N_BX, N_BY, N_BX, MOST, LEAF), jnp.float32)
    delivered = delivered.at[target, row_ids, home_ids, rank].set(leaves)
    return top_out, delivered
```

```python
import jax
import jax.numpy as jnp
from jax import lax
from jax.sharding import PartitionSpec as P

HIGH = lax.Precision.HIGH


def swapped(value, axis):
    pairs = [(source, source ^ 1) for source in range(lax.axis_size(axis))]
    return lax.ppermute(value, axis, pairs)


def product(left, right):
    return jnp.einsum("nij,njk->nik", left, right, precision=HIGH)


def apply_map(matrix, vector):
    return jnp.einsum("nij,nj->ni", matrix, vector, precision=HIGH)


def ordered(parity, mine, other):
    first = jnp.where(parity == 0, mine, other)
    second = jnp.where(parity == 0, other, mine)
    return first, second


def chosen_maps(classes, class_maps):
    levels = class_maps.shape[0]
    onehot = (classes[:, None] == jnp.arange(levels, dtype=jnp.int32)[None, :]).astype(jnp.bfloat16)
    return jnp.einsum(
        "kc,cab->kab", onehot, class_maps, preferred_element_type=jnp.float32
    ).astype(jnp.bfloat16)


def side_of(fields, side, face):
    outer = jnp.where(side == 0, fields[:, : 2 * face], fields[:, 2 * face : 4 * face])
    south = jnp.where(side == 0, fields[:, 4 * face : 5 * face], fields[:, 5 * face : 6 * face])
    north = jnp.where(side == 0, fields[:, 6 * face : 7 * face], fields[:, 7 * face : 8 * face])
    return jnp.concatenate([outer, south, north], axis=1)


def edges(side, outer, inner, south, north):
    west, east = ordered(side, outer, inner)
    return jnp.concatenate([west, east, south, north], axis=1)


def shards(leaf_factor, class_maps, depth_class, owners, top_in):
    factor = leaf_factor[0, 0]
    leaves_here = factor.shape[0]
    face = factor.shape[1] // 4
    half = leaves_here // 2
    quarter = leaves_here // 4
    row = lax.axis_index("by")
    rp = row % 2
    cp = lax.axis_index("bx") % 2
    fields_here = top_in[0, 0]

    got_factor = swapped(lax.dynamic_slice_in_dim(factor, (1 - rp) * half, half, 0), "by")
    got_fields = swapped(side_of(fields_here, 1 - cp, face), "bx")
    mine_factor = lax.dynamic_slice_in_dim(factor, rp * half, half, 0)
    fields = jnp.concatenate(ordered(cp, side_of(fields_here, cp, face), got_fields), axis=0)
    factor_a, factor_b = ordered(rp, mine_factor, got_factor)
    classes = lax.dynamic_slice(depth_class[0], (row - rp, rp * half), (2, half))

    def leaf_maps(own_classes, own_factor):
        chosen = chosen_maps(own_classes, class_maps)
        return jnp.einsum("kab,kbc->kac", chosen, own_factor, preferred_element_type=jnp.float32)

    map_a = leaf_maps(classes[0], factor_a)
    map_b = leaf_maps(classes[1], factor_b)
    nothing = jnp.zeros((half, face), jnp.float32)
    known_a = edges(cp, fields[:, :face], nothing, fields[:, 2 * face : 3 * face], nothing)
    known_b = edges(cp, fields[:, face : 2 * face], nothing, nothing, fields[:, 3 * face :])
    from_a = apply_map(map_a, known_a)
    from_b = apply_map(map_b, known_b)

    def inner_of(value, axis):
        first = lax.slice_in_dim(value, 0, face, axis=axis)
        second = lax.slice_in_dim(value, face, 2 * face, axis=axis)
        return jnp.where(cp == 0, second, first)

    rows_a = map_a[:, 3 * face :]
    rows_b = map_b[:, 2 * face : 3 * face]
    a_ss = rows_a[:, :, 3 * face :]
    b_ss = rows_b[:, :, 2 * face : 3 * face]
    zeros = jnp.zeros((half, face, face), jnp.float32)
    a_si = jnp.concatenate([inner_of(rows_a, 2), zeros, from_a[:, 3 * face :, None]], axis=2)
    b_si = jnp.concatenate(
        [zeros, inner_of(rows_b, 2), from_b[:, 2 * face : 3 * face, None]], axis=2
    )
    both = product(b_ss, jnp.concatenate([a_ss, a_si], axis=2))
    crossed = both[:, :, :face]
    right = both[:, :, face:] - b_si
    inward_a = right + product(crossed, right)
    inward_a = right + product(crossed, inward_a)
    inward_a = right + product(crossed, inward_a)
    inward_b = -a_si - product(a_ss, inward_a)
    inner_a = inner_of(map_a, 1)
    inner_b = inner_of(map_b, 1)
    top_rows = jnp.concatenate(
        [inner_of(inner_a, 2), zeros, inner_of(from_a, 1)[:, :, None]], axis=2
    ) + product(inner_a[:, :, 3 * face :], inward_a)
    low_rows = jnp.concatenate(
        [zeros, inner_of(inner_b, 2), inner_of(from_b, 1)[:, :, None]], axis=2
    ) + product(inner_b[:, :, 2 * face : 3 * face], inward_b)
    level = jnp.concatenate([top_rows, low_rows], axis=1)

    mine_level = lax.dynamic_slice_in_dim(level, cp * quarter, quarter, 0)
    got_level = swapped(lax.dynamic_slice_in_dim(level, (1 - cp) * quarter, quarter, 0), "bx")
    west, east = ordered(cp, mine_level, got_level)
    west_map, west_out = west[:, :, : 2 * face], west[:, :, 2 * face]
    east_map, east_out = east[:, :, : 2 * face], east[:, :, 2 * face]
    start = apply_map(east_map, west_out) - east_out
    inward = start
    for _ in range(3):
        inward = start + apply_map(east_map, apply_map(west_map, inward))
    backward = -west_out - apply_map(west_map, inward)
    kept = jnp.where(cp == 0, inward, backward)
    returned = swapped(jnp.where(cp == 0, backward, inward), "bx")
    inner = jnp.concatenate(ordered(cp, kept, returned), axis=0)

    part_a = apply_map(inward_a[:, :, : 2 * face], inner) + inward_a[:, :, 2 * face]
    part_b = apply_map(inward_b[:, :, : 2 * face], inner) + inward_b[:, :, 2 * face]
    leaf_a = edges(cp, fields[:, :face], inner[:, :face], fields[:, 2 * face : 3 * face], part_a)
    leaf_b = edges(cp, fields[:, face : 2 * face], inner[:, face:], part_b, fields[:, 3 * face :])
    kept_leaves, given_leaves = jnp.where(rp == 0, leaf_a, leaf_b), jnp.where(rp == 0, leaf_b, leaf_a)
    returned_leaves = swapped(given_leaves, "by")
    leaf_fields = jnp.concatenate(ordered(rp, kept_leaves, returned_leaves), axis=0)

    columns = lax.axis_size("bx")
    most = max(2, (3 * leaves_here + 2 * columns - 1) // (2 * columns))
    target = owners[0, 0, :, 0]
    onehot = (target[:, None] == jnp.arange(columns, dtype=jnp.int32)[None, :]).astype(jnp.int32)
    rank = jnp.sum((jnp.cumsum(onehot, axis=0) - onehot) * onehot, axis=1)
    slot = target * most + rank
    selector = (slot[None, :] == jnp.arange(columns * most, dtype=jnp.int32)[:, None]).astype(
        jnp.float32
    )
    outgoing = jnp.dot(selector, leaf_fields, precision=lax.Precision.HIGHEST).reshape(
        columns, most, leaf_fields.shape[1]
    )
    arrived = lax.all_to_all(outgoing, "bx", split_axis=0, concat_axis=0, tiled=True)

    out_a = apply_map(map_a, leaf_a)
    out_b = apply_map(map_b, leaf_b)

    def outer_of(value):
        return jnp.where(cp == 0, value[:, :face], value[:, face : 2 * face])

    out = jnp.concatenate(
        [outer_of(out_a), outer_of(out_b), out_a[:, 2 * face : 3 * face], out_b[:, 3 * face :]],
        axis=1,
    )
    mine_out = lax.dynamic_slice_in_dim(out, cp * quarter, quarter, 0)
    got_out = swapped(lax.dynamic_slice_in_dim(out, (1 - cp) * quarter, quarter, 0), "bx")
    west_out, east_out = ordered(cp, mine_out, got_out)
    top_out = jnp.concatenate(
        [
            west_out[:, : 2 * face],
            east_out[:, : 2 * face],
            west_out[:, 2 * face : 3 * face],
            east_out[:, 2 * face : 3 * face],
            west_out[:, 3 * face :],
            east_out[:, 3 * face :],
        ],
        axis=1,
    )
    return (top_out[None, None], arrived[None, None])


def solution(mesh):
    placed = (
        P("bx", "by", "seastate", None, None),
        P("seastate", None, None),
        P("bx", None, "seastate"),
        P("bx", "by", "seastate", None),
        P("bx", "by", "seastate", None),
    )
    return jax.shard_map(
        shards,
        mesh=mesh,
        in_specs=placed,
        out_specs=(P("bx", "by", "seastate", None), P("bx", "by", None, "seastate", None)),
        check_vma=False,
    )
```

```python
import functools

import jax
import jax.numpy as jnp
from jax import lax
from jax.experimental import pallas as pl
from jax.experimental.pallas import tpu as pltpu
from jax.sharding import PartitionSpec as P

MESH = pl.DeviceIdType.MESH
F32 = jnp.float32
BF16 = jnp.bfloat16


def halves(value):
    high = value.astype(BF16)
    return high, (value - high.astype(F32)).astype(BF16)


def product(left, right):
    left_high, left_low = halves(left)
    right_high, right_low = halves(right)
    return jnp.dot(
        jnp.concatenate([left_high, left_high, left_low], axis=1),
        jnp.concatenate([right_high, right_low, right_high], axis=0),
        preferred_element_type=F32,
    )


def kernel(
    columns,
    most,
    classes_ref,
    factor_ref,
    maps_ref,
    owners_ref,
    top_ref,
    out_ref,
    delivered_ref,
    factors,
    leaf_maps,
    inward,
    blocks,
    answers,
    fields,
    fields_out,
    transposed,
    opened,
    inner,
    inner_out,
    leaves,
    home,
    outgoing,
    arrived,
    outs,
    outs_out,
    local_sem,
    factor_send,
    factor_recv,
    field_sem,
    block_send,
    block_recv,
    answer_sem,
    inner_sem,
    leaf_sem,
    outs_sem,
    all_send,
    all_recv,
):
    leaves_here, leaf = factor_ref.shape[0], factor_ref.shape[1]
    face = leaf // 4
    half, quarter = leaves_here // 2, leaves_here // 4
    pairs = quarter // 2
    row, column = lax.axis_index("by"), lax.axis_index("bx")
    rp, cp = lax.rem(row, 2), lax.rem(column, 2)
    row_mate, column_mate = row + 1 - 2 * rp, column + 1 - 2 * cp
    first, second = (1 - cp) * quarter, cp * quarter
    west = cp == 0

    def to_row_mate(source, target, send, recv):
        return pltpu.make_async_remote_copy(
            src_ref=source, dst_ref=target, send_sem=send, recv_sem=recv,
            device_id={"by": row_mate}, device_id_type=MESH,
        )

    def to_column_mate(source, target, send, recv):
        return pltpu.make_async_remote_copy(
            src_ref=source, dst_ref=target, send_sem=send, recv_sem=recv,
            device_id={"bx": column_mate}, device_id_type=MESH,
        )

    own_copies, mate_copies = [], []
    for index, begin in enumerate((first, second)):
        own = pltpu.make_async_copy(
            factor_ref.at[pl.ds(rp * half + begin, quarter)],
            factors.at[rp, pl.ds(begin, quarter)],
            local_sem.at[index],
        )
        own.start()
        own_copies.append(own)
        mate_copies.append(
            to_row_mate(
                factor_ref.at[pl.ds((1 - rp) * half + begin, quarter)],
                factors.at[rp, pl.ds(begin, quarter)],
                factor_send.at[index],
                factor_recv.at[index],
            )
        )

    barrier = pltpu.get_barrier_semaphore()
    pl.semaphore_signal(barrier, inc=1, device_id={"by": row_mate}, device_id_type=MESH)
    for step in range(1, columns):
        pl.semaphore_signal(
            barrier, inc=1, device_id={"bx": lax.rem(column + step, columns)}, device_id_type=MESH
        )
    pl.semaphore_wait(barrier, columns)
    for copy in mate_copies:
        copy.start()

    top = top_ref[...]
    none = jnp.zeros((quarter, face), F32)

    def part(index):
        return top[:, index * face : (index + 1) * face]

    def row_of(*parts):
        return jnp.concatenate(parts, axis=1)

    sides = (
        (row_of(part(0), none, part(4), none), row_of(part(1), none, none, part(6))),
        (row_of(none, part(2), part(5), none), row_of(none, part(3), none, part(7))),
    )
    for index in range(2):
        mine = jnp.where(west, sides[0][index], sides[1][index])
        other = jnp.where(west, sides[1][index], sides[0][index])
        for box in range(quarter):
            fields[cp, index, box] = mine[box : box + 1]
            fields_out[index, box] = other[box : box + 1]
    field_copy = to_column_mate(fields_out, fields.at[cp], field_sem.at[0], field_sem.at[1])
    field_copy.start()

    sub_face = lax.broadcasted_iota(jnp.int32, (face, face), 0)
    lane_face = lax.broadcasted_iota(jnp.int32, (face, face), 1)
    identity = (sub_face == lane_face).astype(F32)
    sub_two = lax.broadcasted_iota(jnp.int32, (2 * face, leaf), 0)
    lane_two = lax.broadcasted_iota(jnp.int32, (2 * face, leaf), 1)
    no_map = jnp.zeros((face, leaf), F32)

    def block_copy(step):
        return to_column_mate(
            blocks.at[0, pl.ds(2 * step, 2)],
            blocks.at[1 + cp, pl.ds(2 * step, 2)],
            block_send.at[step],
            block_recv.at[step],
        )

    def inner_rows(matrix):
        return jnp.where(west, matrix[face : 2 * face], matrix[:face])

    def upward(turn, carry):
        stage, step = turn // 4, lax.rem(turn, 4)
        side = jnp.where(turn < 4, 1 - cp, cp)

        @pl.when(step == 0)
        def _():
            @pl.when(stage == 0)
            def _():
                own_copies[0].wait()
                mate_copies[0].wait_recv()
                field_copy.wait_recv()

            @pl.when(stage == 1)
            def _():
                own_copies[1].wait()
                mate_copies[1].wait_recv()

        slot = jnp.where(turn < 4, 0, 1 + cp)
        boxes = [2 * step, 2 * step + 1, 2 * step + pairs, 2 * step + 1 + pairs]
        places = [side * quarter + box for box in boxes]
        maps_a, maps_b = [], []
        for place in places:
            class_a = classes_ref[row - rp, rp * half + place]
            class_b = classes_ref[row - rp + 1, rp * half + place]
            map_a = jnp.dot(maps_ref[class_a], factors[0, place], preferred_element_type=F32)
            map_b = jnp.dot(maps_ref[class_b], factors[1, place], preferred_element_type=F32)
            leaf_maps[0, place] = map_a
            leaf_maps[1, place] = map_b
            maps_a.append(map_a)
            maps_b.append(map_b)
        rows_a = [m[3 * face :] for m in maps_a]
        rows_b = [m[2 * face : 3 * face] for m in maps_b]
        a_ss = [m[:, 3 * face :] for m in rows_a]
        b_ss = [m[:, 2 * face : 3 * face] for m in rows_b]
        crossed_rows = [product(b, a) for b, a in zip(b_ss, rows_a)]
        crossed = [m[:, 3 * face :] for m in crossed_rows]
        squares = [product(m, m) for m in crossed]
        inverses = [product(identity + m, identity + s) for m, s in zip(crossed, squares)]
        inward_a = [
            product(w, jnp.concatenate([c, -b], axis=1))
            for w, c, b in zip(inverses, crossed_rows, rows_b)
        ]
        inner_a = [inner_rows(m) for m in maps_a]
        inner_b = [inner_rows(m) for m in maps_b]
        spread = [
            product(jnp.concatenate([s, i[:, 3 * face :]], axis=0), x)
            for s, i, x in zip(a_ss, inner_a, inward_a)
        ]
        inward_b = [
            -jnp.concatenate([a, no_map], axis=1) - s[:face] for a, s in zip(rows_a, spread)
        ]
        upper = [
            jnp.concatenate([i, no_map], axis=1) + s[face:] for i, s in zip(inner_a, spread)
        ]
        lower = [
            jnp.concatenate([no_map, i], axis=1) + product(i[:, 2 * face : 3 * face], y)
            for i, y in zip(inner_b, inward_b)
        ]
        packed = []
        for index, (box, place) in enumerate(zip(boxes, places)):
            inward[place, :face] = inward_a[index]
            inward[place, face:] = inward_b[index]
            level = jnp.concatenate([upper[index], lower[index]], axis=0)
            field_a, field_b = fields[side, 0, box], fields[side, 1, box]
            answer = jnp.sum(
                level[:, :leaf] * field_a + level[:, leaf:] * field_b, axis=1, keepdims=True
            )
            answers[slot, box] = jnp.sum(
                jnp.where(sub_two == lane_two, answer, 0.0), axis=0, keepdims=True
            )
            offset = 2 * face * (index // 2)
            shift = offset - face * (1 - cp) + leaf
            moved_a = pltpu.roll(level[:, :leaf], lax.rem(shift, leaf), 1)
            moved_b = pltpu.roll(level[:, leaf:], lax.rem(shift + face, leaf), 1)
            packed.append(jnp.where(lane_two < offset + face, moved_a, moved_b))
        for index in range(2):
            blocks[slot, 2 * step + index] = jnp.where(
                lane_two < 2 * face, packed[index], packed[index + 2]
            )

        @pl.when(stage == 0)
        def _():
            block_copy(step).start()

        return carry

    lax.fori_loop(0, 8, upward, 0)
    answer_copy = to_column_mate(
        answers.at[0], answers.at[1 + cp], answer_sem.at[0], answer_sem.at[1]
    )
    answer_copy.start()

    target = owners_ref[...]
    named = (lax.broadcasted_iota(jnp.int32, (columns, leaves_here), 0) == target).astype(F32)
    before = lax.broadcasted_iota(jnp.int32, (leaves_here, leaves_here), 0) < (
        lax.broadcasted_iota(jnp.int32, (leaves_here, leaves_here), 1)
    )
    earlier = jnp.dot(
        named.astype(BF16), before.astype(F32).astype(BF16), preferred_element_type=F32
    )
    rank = jnp.sum(named * earlier, axis=0, keepdims=True)
    slots = target.astype(F32) * most + rank
    wanted = lax.broadcasted_iota(jnp.int32, (columns * most, leaves_here), 0).astype(F32)
    selector = (wanted == slots).astype(F32).astype(BF16)

    for step in range(4):
        block_copy(step).wait_recv()
    answer_copy.wait_recv()
    for index in range(pairs):
        both = blocks[1, index].T
        transposed[index] = both[: 2 * face]
        transposed[index + pairs] = both[2 * face :]
        other = blocks[2, index]
        opened[index] = other[:, : 2 * face]
        opened[index + pairs] = other[:, 2 * face :]
    diagonal = (
        lax.broadcasted_iota(jnp.int32, (quarter, 2 * face, 2 * face), 1)
        == lax.broadcasted_iota(jnp.int32, (quarter, 2 * face, 2 * face), 2)
    )
    west_out = answers[1][:, :, : 2 * face]
    east_out = answers[2][:, :, : 2 * face]
    start = jnp.sum(
        opened[...] * west_out - jnp.where(diagonal, east_out, 0.0), axis=2, keepdims=True
    )
    value = start
    for _ in range(3):
        between = jnp.sum(transposed[...] * value, axis=1, keepdims=True)
        value = start + jnp.sum(opened[...] * between, axis=2, keepdims=True)
    to_west = jnp.sum(jnp.where(diagonal, value, 0.0), axis=1, keepdims=True)
    to_east = -west_out - jnp.sum(transposed[...] * value, axis=1, keepdims=True)
    gap = jnp.zeros((quarter, 1, face), F32)
    gaps = jnp.zeros((quarter, 1, 2 * face), F32)
    west_rows = (
        jnp.concatenate([gap, to_west[:, :, :face], gaps], axis=2),
        jnp.concatenate([gap, to_west[:, :, face:], gaps], axis=2),
    )
    east_rows = (
        jnp.concatenate([to_east[:, :, :face], gap, gaps], axis=2),
        jnp.concatenate([to_east[:, :, face:], gap, gaps], axis=2),
    )
    for index in range(2):
        inner[cp, index] = jnp.where(west, west_rows[index], east_rows[index])
        inner_out[index] = jnp.where(west, east_rows[index], west_rows[index])
    inner_copy = to_column_mate(inner_out, inner.at[cp], inner_sem.at[0], inner_sem.at[1])
    inner_copy.start()

    sub_row = lax.broadcasted_iota(jnp.int32, (face, leaf), 0)
    lane_row = lax.broadcasted_iota(jnp.int32, (face, leaf), 1)

    def downward(turn, carry):
        side = jnp.where(turn < 4, cp, 1 - cp)

        @pl.when(turn == 4)
        def _():
            inner_copy.wait_recv()

        for index in range(4):
            box = lax.rem(turn, 4) * 4 + index
            place = side * quarter + box
            field_a = fields[side, 0, box] + inner[side, 0, box]
            field_b = fields[side, 1, box] + inner[side, 1, box]
            both = inward[place]
            found = jnp.sum(
                both[:, :leaf] * field_a + both[:, leaf:] * field_b, axis=1, keepdims=True
            )
            north = jnp.where(lane_row == sub_row + 3 * face, found[:face], 0.0)
            south = jnp.where(lane_row == sub_row + 2 * face, found[face:], 0.0)
            leaves[0, pl.ds(place, 1)] = field_a + jnp.sum(north, axis=0, keepdims=True)
            leaves[1, pl.ds(place, 1)] = field_b + jnp.sum(south, axis=0, keepdims=True)
        return carry

    lax.fori_loop(0, 8, downward, 0)
    leaf_copy = to_row_mate(leaves.at[1 - rp], home.at[rp], leaf_sem.at[0], leaf_sem.at[1])
    leaf_copy.start()
    home[rp] = leaves[rp]

    sub_all = lax.broadcasted_iota(jnp.int32, (leaf, leaf), 0)
    lane_all = lax.broadcasted_iota(jnp.int32, (leaf, leaf), 1)

    def outward(side, target_ref):
        def body(turn, carry):
            for index in range(4):
                box = turn * 4 + index
                place = side * quarter + box
                leaf_a = leaves[0, pl.ds(place, 1)]
                leaf_b = leaves[1, pl.ds(place, 1)]
                outer = pl.ds(cp * face, face)
                found = jnp.concatenate(
                    [
                        leaf_maps[0, place, outer] * leaf_a,
                        leaf_maps[1, place, outer] * leaf_b,
                        leaf_maps[0, place, 2 * face : 3 * face] * leaf_a,
                        leaf_maps[1, place, 3 * face :] * leaf_b,
                    ],
                    axis=0,
                )
                found = jnp.sum(found, axis=1, keepdims=True)
                target_ref[pl.ds(box, 1)] = jnp.sum(
                    jnp.where(sub_all == lane_all, found, 0.0), axis=0, keepdims=True
                )
            return carry

        lax.fori_loop(0, quarter // 4, body, 0)

    outward(1 - cp, outs_out)
    outs_copy = to_column_mate(outs_out, outs.at[cp], outs_sem.at[0], outs_sem.at[1])
    outs_copy.start()

    leaf_copy.wait_recv()
    values = jnp.concatenate([home[0], home[1]], axis=0)
    high, rest = halves(values)
    middle, low = halves(values - high.astype(F32))
    chosen = (
        jnp.dot(selector, high, preferred_element_type=F32)
        + jnp.dot(selector, middle, preferred_element_type=F32)
        + jnp.dot(selector, low, preferred_element_type=F32)
    )
    for owner in range(columns):
        outgoing[owner] = chosen[owner * most : (owner + 1) * most]
    all_copies = []
    for step in range(1, columns):
        owner = lax.rem(column + step, columns)
        copy = pltpu.make_async_remote_copy(
            src_ref=outgoing.at[owner],
            dst_ref=arrived.at[column],
            send_sem=all_send.at[step - 1],
            recv_sem=all_recv.at[step - 1],
            device_id={"bx": owner},
            device_id_type=MESH,
        )
        copy.start()
        all_copies.append(copy)
    arrived[column] = outgoing[column]

    outward(cp, outs.at[cp])
    outs_copy.wait_recv()
    out_west, out_east = outs[0], outs[1]
    out_ref[...] = jnp.concatenate(
        [
            out_west[:, : 2 * face],
            out_east[:, : 2 * face],
            out_west[:, 2 * face : 3 * face],
            out_east[:, 2 * face : 3 * face],
            out_west[:, 3 * face :],
            out_east[:, 3 * face :],
        ],
        axis=1,
    )
    for copy in all_copies:
        copy.wait_recv()
    delivered_ref[...] = arrived[...]

    for copy in mate_copies + all_copies:
        copy.wait_send()
    for copy in (field_copy, answer_copy, inner_copy, leaf_copy, outs_copy):
        copy.wait_send()
    for step in range(4):
        block_copy(step).wait_send()


def shards(leaf_factor, class_maps, depth_class, owners, top_in):
    factor = leaf_factor[0, 0]
    leaves_here, leaf = factor.shape[0], factor.shape[1]
    half, quarter = leaves_here // 2, leaves_here // 4
    inside = leaf // 2
    columns = lax.axis_size("bx")
    most = max(2, (3 * leaves_here + 2 * columns - 1) // (2 * columns))
    whole = pl.BlockSpec(memory_space=pltpu.VMEM)
    top_out, arrived = pl.pallas_call(
        functools.partial(kernel, columns, most),
        out_shape=(
            jax.ShapeDtypeStruct((quarter, 2 * leaf), F32),
            jax.ShapeDtypeStruct((columns, most, leaf), F32),
        ),
        in_specs=[
            pl.BlockSpec(memory_space=pltpu.SMEM),
            pl.BlockSpec(memory_space=pl.ANY),
            whole,
            whole,
            whole,
        ],
        out_specs=(whole, whole),
        scratch_shapes=[
            pltpu.VMEM((2, half, leaf, leaf), BF16),
            pltpu.VMEM((2, half, leaf, leaf), F32),
            pltpu.VMEM((half, inside, 2 * leaf), F32),
            pltpu.VMEM((3, quarter // 2, inside, leaf), F32),
            pltpu.VMEM((3, quarter, 1, leaf), F32),
            pltpu.VMEM((2, 2, quarter, 1, leaf), F32),
            pltpu.VMEM((2, quarter, 1, leaf), F32),
            pltpu.VMEM((quarter, inside, inside), F32),
            pltpu.VMEM((quarter, inside, inside), F32),
            pltpu.VMEM((2, 2, quarter, 1, leaf), F32),
            pltpu.VMEM((2, quarter, 1, leaf), F32),
            pltpu.VMEM((2, half, leaf), F32),
            pltpu.VMEM((2, half, leaf), F32),
            pltpu.VMEM((columns, most, leaf), F32),
            pltpu.VMEM((columns, most, leaf), F32),
            pltpu.VMEM((2, quarter, leaf), F32),
            pltpu.VMEM((quarter, leaf), F32),
            pltpu.SemaphoreType.DMA((2,)),
            pltpu.SemaphoreType.DMA((2,)),
            pltpu.SemaphoreType.DMA((2,)),
            pltpu.SemaphoreType.DMA((2,)),
            pltpu.SemaphoreType.DMA((4,)),
            pltpu.SemaphoreType.DMA((4,)),
            pltpu.SemaphoreType.DMA((2,)),
            pltpu.SemaphoreType.DMA((2,)),
            pltpu.SemaphoreType.DMA((2,)),
            pltpu.SemaphoreType.DMA((2,)),
            pltpu.SemaphoreType.DMA((columns - 1,)),
            pltpu.SemaphoreType.DMA((columns - 1,)),
        ],
        compiler_params=pltpu.CompilerParams(
            collective_id=0, has_side_effects=True, vmem_limit_bytes=40 * 1024 * 1024
        ),
    )(depth_class[0], factor, class_maps, owners[0, 0].reshape(1, leaves_here), top_in[0, 0])
    return (top_out[None, None], arrived[None, None])


def solution(mesh):
    placed = (
        P("bx", "by", "seastate", None, None),
        P("seastate", None, None),
        P("bx", None, "seastate"),
        P("bx", "by", "seastate", None),
        P("bx", "by", "seastate", None),
    )
    return jax.shard_map(
        shards,
        mesh=mesh,
        in_specs=placed,
        out_specs=(P("bx", "by", "seastate", None), P("bx", "by", None, "seastate", None)),
        check_vma=False,
    )
```

```python
import functools

import jax
import jax.numpy as jnp
from jax import lax
from jax.experimental import pallas as pl
from jax.experimental.pallas import tpu as pltpu
from jax.sharding import PartitionSpec as P

MESH = pl.DeviceIdType.MESH
F32 = jnp.float32
BF16 = jnp.bfloat16
GROUP = 8


def halves(value):
    high = value.astype(BF16)
    return high, (value - high.astype(F32)).astype(BF16)


def product(left, right):
    left_high, left_low = halves(left)
    right_high, right_low = halves(right)
    return jnp.dot(
        jnp.concatenate([left_high, left_high, left_low], axis=1),
        jnp.concatenate([right_high, right_low, right_high], axis=0),
        preferred_element_type=F32,
    )


def kernel(
    columns,
    most,
    classes_hbm,
    factor_ref,
    maps_hbm,
    owners_hbm,
    top_hbm,
    out_ref,
    delivered_ref,
    classes_ref,
    maps_ref,
    owners_ref,
    top_ref,
    factors,
    leaf_maps,
    inward,
    blocks,
    answers,
    fields,
    fields_out,
    transposed,
    opened,
    inner,
    inner_out,
    leaves,
    home,
    outgoing,
    outs,
    outs_out,
    result,
    operand_sem,
    result_sem,
    local_sem,
    factor_send,
    factor_recv,
    field_sem,
    block_send,
    block_recv,
    answer_sem,
    inner_sem,
    leaf_sem,
    outs_sem,
    all_send,
    all_recv,
):
    leaves_here, leaf = factor_ref.shape[0], factor_ref.shape[1]
    face = leaf // 4
    half, quarter = leaves_here // 2, leaves_here // 4
    pairs = quarter // 2
    per_stage = quarter // GROUP
    turns = 2 * per_stage
    row, column = lax.axis_index("by"), lax.axis_index("bx")
    rp, cp = lax.rem(row, 2), lax.rem(column, 2)
    row_mate, column_mate = row + 1 - 2 * rp, column + 1 - 2 * cp
    first, second = (1 - cp) * quarter, cp * quarter
    west = cp == 0

    def to_row_mate(source, target, send, recv):
        return pltpu.make_async_remote_copy(
            src_ref=source, dst_ref=target, send_sem=send, recv_sem=recv,
            device_id={"by": row_mate}, device_id_type=MESH,
        )

    def to_column_mate(source, target, send, recv):
        return pltpu.make_async_remote_copy(
            src_ref=source, dst_ref=target, send_sem=send, recv_sem=recv,
            device_id={"bx": column_mate}, device_id_type=MESH,
        )

    operands = [
        pltpu.make_async_copy(source, target, operand_sem.at[index])
        for index, (source, target) in enumerate(
            (
                (top_hbm, top_ref),
                (classes_hbm, classes_ref),
                (maps_hbm, maps_ref),
                (owners_hbm, owners_ref),
            )
        )
    ]
    for copy in operands:
        copy.start()
    own_copies, mate_copies = [], []
    begins = [start + GROUP * index for start in (first, second) for index in range(per_stage)]
    for index, begin in enumerate(begins):
        own = pltpu.make_async_copy(
            factor_ref.at[pl.ds(rp * half + begin, GROUP)],
            factors.at[rp, pl.ds(begin, GROUP)],
            local_sem.at[index],
        )
        own.start()
        own_copies.append(own)
        mate_copies.append(
            to_row_mate(
                factor_ref.at[pl.ds((1 - rp) * half + begin, GROUP)],
                factors.at[rp, pl.ds(begin, GROUP)],
                factor_send.at[index],
                factor_recv.at[index],
            )
        )

    barrier = pltpu.get_barrier_semaphore()
    pl.semaphore_signal(barrier, inc=1, device_id={"by": row_mate}, device_id_type=MESH)
    for step in range(1, columns):
        pl.semaphore_signal(
            barrier, inc=1, device_id={"bx": lax.rem(column + step, columns)}, device_id_type=MESH
        )
    pl.semaphore_wait(barrier, columns)
    for copy in mate_copies:
        copy.start()

    operands[0].wait()
    top = top_ref[...]
    none = jnp.zeros((quarter, face), F32)

    def part(index):
        return top[:, index * face : (index + 1) * face]

    def row_of(*parts):
        return jnp.concatenate(parts, axis=1)

    sides = (
        (row_of(part(0), none, part(4), none), row_of(part(1), none, none, part(6))),
        (row_of(none, part(2), part(5), none), row_of(none, part(3), none, part(7))),
    )
    for index in range(2):
        mine = jnp.where(west, sides[0][index], sides[1][index])
        other = jnp.where(west, sides[1][index], sides[0][index])
        for box in range(quarter):
            fields[cp, index, box] = mine[box : box + 1]
            fields_out[index, box] = other[box : box + 1]
    field_copy = to_column_mate(fields_out, fields.at[cp], field_sem.at[0], field_sem.at[1])
    field_copy.start()

    sub_face = lax.broadcasted_iota(jnp.int32, (face, face), 0)
    lane_face = lax.broadcasted_iota(jnp.int32, (face, face), 1)
    identity = (sub_face == lane_face).astype(F32)
    sub_two = lax.broadcasted_iota(jnp.int32, (2 * face, leaf), 0)
    lane_two = lax.broadcasted_iota(jnp.int32, (2 * face, leaf), 1)
    no_map = jnp.zeros((face, leaf), F32)

    def block_copy(step):
        return to_column_mate(
            blocks.at[0, pl.ds(step * (GROUP // 2), GROUP // 2)],
            blocks.at[1 + cp, pl.ds(step * (GROUP // 2), GROUP // 2)],
            block_send.at[step],
            block_recv.at[step],
        )

    def inner_rows(matrix):
        return jnp.where(west, matrix[face : 2 * face], matrix[:face])

    def upward(turn, carry):
        stage, step = turn // per_stage, lax.rem(turn, per_stage)
        side = jnp.where(stage == 0, 1 - cp, cp)
        slot = jnp.where(stage == 0, 0, 1 + cp)
        for index in range(turns):

            @pl.when(turn == index)
            def _():
                own_copies[index].wait()
                mate_copies[index].wait_recv()

        boxes = [step * GROUP + index for index in range(GROUP)]
        places = [side * quarter + box for box in boxes]
        maps_a, maps_b = [], []
        for place in places:
            class_a = classes_ref[row - rp, rp * half + place]
            class_b = classes_ref[row - rp + 1, rp * half + place]
            map_a = jnp.dot(maps_ref[class_a], factors[0, place], preferred_element_type=F32)
            map_b = jnp.dot(maps_ref[class_b], factors[1, place], preferred_element_type=F32)
            leaf_maps[0, place] = map_a
            leaf_maps[1, place] = map_b
            maps_a.append(map_a)
            maps_b.append(map_b)
        rows_a = [m[3 * face :] for m in maps_a]
        rows_b = [m[2 * face : 3 * face] for m in maps_b]
        inner_a = [inner_rows(m) for m in maps_a]
        inner_b = [inner_rows(m) for m in maps_b]
        firsts = [
            product(jnp.concatenate([b, i], axis=0)[:, 2 * face : 3 * face], a)
            for b, i, a in zip(rows_b, inner_b, rows_a)
        ]
        starts = [jnp.concatenate([f[:face], -b], axis=1) for f, b in zip(firsts, rows_b)]
        lefts = [
            jnp.concatenate([f[:face], a, i, f[face:]], axis=0)[:, 3 * face :]
            for f, a, i in zip(firsts, rows_a, inner_a)
        ]
        seconds = [product(left, left[:face]) for left in lefts]
        rights = [st + product(sec[:face], st) for st, sec in zip(starts, seconds)]
        spreads = [
            product(
                jnp.concatenate([identity + left[:face], left[face:] + sec[face:]], axis=0), right
            )
            for left, sec, right in zip(lefts, seconds, rights)
        ]
        inward_a = [sp[:face] for sp in spreads]
        inward_b = [
            -jnp.concatenate([a, no_map], axis=1) - sp[face : 2 * face]
            for a, sp in zip(rows_a, spreads)
        ]
        upper = [
            jnp.concatenate([i, no_map], axis=1) + sp[2 * face : 3 * face]
            for i, sp in zip(inner_a, spreads)
        ]
        lower = [
            jnp.concatenate([-f[face:], i], axis=1) - sp[3 * face :]
            for f, i, sp in zip(firsts, inner_b, spreads)
        ]
        packed = []
        for index, (box, place) in enumerate(zip(boxes, places)):
            inward[place, :face] = inward_a[index]
            inward[place, face:] = inward_b[index]
            level = jnp.concatenate([upper[index], lower[index]], axis=0)
            field_a, field_b = fields[side, 0, box], fields[side, 1, box]
            answer = jnp.sum(
                level[:, :leaf] * field_a + level[:, leaf:] * field_b, axis=1, keepdims=True
            )
            answers[slot, box] = jnp.sum(
                jnp.where(sub_two == lane_two, answer, 0.0), axis=0, keepdims=True
            )
            offset = 2 * face * (index % 2)
            shift = offset - face * (1 - cp) + leaf
            moved_a = pltpu.roll(level[:, :leaf], lax.rem(shift, leaf), 1)
            moved_b = pltpu.roll(level[:, leaf:], lax.rem(shift + face, leaf), 1)
            packed.append(jnp.where(lane_two < offset + face, moved_a, moved_b))
        for index in range(GROUP // 2):
            blocks[slot, step * (GROUP // 2) + index] = jnp.where(
                lane_two < 2 * face, packed[2 * index], packed[2 * index + 1]
            )

        @pl.when(stage == 0)
        def _():
            block_copy(step).start()

        return carry

    operands[1].wait()
    operands[2].wait()
    field_copy.wait_recv()
    lax.fori_loop(0, turns, upward, 0)
    answer_copy = to_column_mate(
        answers.at[0], answers.at[1 + cp], answer_sem.at[0], answer_sem.at[1]
    )
    answer_copy.start()

    operands[3].wait()
    target = owners_ref[...]
    named = (lax.broadcasted_iota(jnp.int32, (columns, leaves_here), 0) == target).astype(F32)
    before = lax.broadcasted_iota(jnp.int32, (leaves_here, leaves_here), 0) < (
        lax.broadcasted_iota(jnp.int32, (leaves_here, leaves_here), 1)
    )
    earlier = jnp.dot(
        named.astype(BF16), before.astype(F32).astype(BF16), preferred_element_type=F32
    )
    rank = jnp.sum(named * earlier, axis=0, keepdims=True)
    slots = target.astype(F32) * most + rank
    wanted = lax.broadcasted_iota(jnp.int32, (columns * most, leaves_here), 0).astype(F32)
    selector = (wanted == slots).astype(F32).astype(BF16)

    for step in range(per_stage):
        block_copy(step).wait_recv()
    answer_copy.wait_recv()
    for index in range(pairs):
        both = blocks[1, index].T
        transposed[2 * index] = both[: 2 * face]
        transposed[2 * index + 1] = both[2 * face :]
        other = blocks[2, index]
        opened[2 * index] = other[:, : 2 * face]
        opened[2 * index + 1] = other[:, 2 * face :]
    diagonal = (
        lax.broadcasted_iota(jnp.int32, (quarter, 2 * face, 2 * face), 1)
        == lax.broadcasted_iota(jnp.int32, (quarter, 2 * face, 2 * face), 2)
    )
    west_out = answers[1][:, :, : 2 * face]
    east_out = answers[2][:, :, : 2 * face]
    start = jnp.sum(
        opened[...] * west_out - jnp.where(diagonal, east_out, 0.0), axis=2, keepdims=True
    )
    value = start
    for _ in range(3):
        between = jnp.sum(transposed[...] * value, axis=1, keepdims=True)
        value = start + jnp.sum(opened[...] * between, axis=2, keepdims=True)
    to_west = jnp.sum(jnp.where(diagonal, value, 0.0), axis=1, keepdims=True)
    to_east = -west_out - jnp.sum(transposed[...] * value, axis=1, keepdims=True)
    gap = jnp.zeros((quarter, 1, face), F32)
    gaps = jnp.zeros((quarter, 1, 2 * face), F32)
    west_rows = (
        jnp.concatenate([gap, to_west[:, :, :face], gaps], axis=2),
        jnp.concatenate([gap, to_west[:, :, face:], gaps], axis=2),
    )
    east_rows = (
        jnp.concatenate([to_east[:, :, :face], gap, gaps], axis=2),
        jnp.concatenate([to_east[:, :, face:], gap, gaps], axis=2),
    )
    for index in range(2):
        inner[cp, index] = jnp.where(west, west_rows[index], east_rows[index])
        inner_out[index] = jnp.where(west, east_rows[index], west_rows[index])
    inner_copy = to_column_mate(inner_out, inner.at[cp], inner_sem.at[0], inner_sem.at[1])
    inner_copy.start()

    sub_row = lax.broadcasted_iota(jnp.int32, (face, leaf), 0)
    lane_row = lax.broadcasted_iota(jnp.int32, (face, leaf), 1)

    def downward(turn, carry):
        side = jnp.where(turn < 4, cp, 1 - cp)

        @pl.when(turn == 4)
        def _():
            inner_copy.wait_recv()

        for index in range(4):
            box = lax.rem(turn, 4) * 4 + index
            place = side * quarter + box
            field_a = fields[side, 0, box] + inner[side, 0, box]
            field_b = fields[side, 1, box] + inner[side, 1, box]
            both = inward[place]
            found = jnp.sum(
                both[:, :leaf] * field_a + both[:, leaf:] * field_b, axis=1, keepdims=True
            )
            north = jnp.where(lane_row == sub_row + 3 * face, found[:face], 0.0)
            south = jnp.where(lane_row == sub_row + 2 * face, found[face:], 0.0)
            leaves[0, pl.ds(place, 1)] = field_a + jnp.sum(north, axis=0, keepdims=True)
            leaves[1, pl.ds(place, 1)] = field_b + jnp.sum(south, axis=0, keepdims=True)
        return carry

    lax.fori_loop(0, 8, downward, 0)
    leaf_copy = to_row_mate(leaves.at[1 - rp], home.at[rp], leaf_sem.at[0], leaf_sem.at[1])
    leaf_copy.start()
    home[rp] = leaves[rp]

    sub_all = lax.broadcasted_iota(jnp.int32, (leaf, leaf), 0)
    lane_all = lax.broadcasted_iota(jnp.int32, (leaf, leaf), 1)

    def outward(side, target_ref):
        def body(turn, carry):
            for index in range(4):
                box = turn * 4 + index
                place = side * quarter + box
                leaf_a = leaves[0, pl.ds(place, 1)]
                leaf_b = leaves[1, pl.ds(place, 1)]
                outer = pl.ds(cp * face, face)
                found = jnp.concatenate(
                    [
                        leaf_maps[0, place, outer] * leaf_a,
                        leaf_maps[1, place, outer] * leaf_b,
                        leaf_maps[0, place, 2 * face : 3 * face] * leaf_a,
                        leaf_maps[1, place, 3 * face :] * leaf_b,
                    ],
                    axis=0,
                )
                found = jnp.sum(found, axis=1, keepdims=True)
                target_ref[pl.ds(box, 1)] = jnp.sum(
                    jnp.where(sub_all == lane_all, found, 0.0), axis=0, keepdims=True
                )
            return carry

        lax.fori_loop(0, quarter // 4, body, 0)

    outward(1 - cp, outs_out)
    outs_copy = to_column_mate(outs_out, outs.at[cp], outs_sem.at[0], outs_sem.at[1])
    outs_copy.start()

    leaf_copy.wait_recv()
    values = jnp.concatenate([home[0], home[1]], axis=0)
    high, rest = halves(values)
    middle, low = halves(values - high.astype(F32))
    chosen = (
        jnp.dot(selector, high, preferred_element_type=F32)
        + jnp.dot(selector, middle, preferred_element_type=F32)
        + jnp.dot(selector, low, preferred_element_type=F32)
    )
    for owner in range(columns):
        outgoing[owner] = chosen[owner * most : (owner + 1) * most]
    all_copies = []
    for step in range(1, columns):
        owner = lax.rem(column + step, columns)
        copy = pltpu.make_async_remote_copy(
            src_ref=outgoing.at[owner],
            dst_ref=delivered_ref.at[column],
            send_sem=all_send.at[step - 1],
            recv_sem=all_recv.at[step - 1],
            device_id={"bx": owner},
            device_id_type=MESH,
        )
        copy.start()
        all_copies.append(copy)
    keep = pltpu.make_async_copy(
        outgoing.at[column], delivered_ref.at[column], result_sem.at[0]
    )
    keep.start()

    outward(cp, outs.at[cp])
    outs_copy.wait_recv()
    out_west, out_east = outs[0], outs[1]
    result[...] = jnp.concatenate(
        [
            out_west[:, : 2 * face],
            out_east[:, : 2 * face],
            out_west[:, 2 * face : 3 * face],
            out_east[:, 2 * face : 3 * face],
            out_west[:, 3 * face :],
            out_east[:, 3 * face :],
        ],
        axis=1,
    )
    result_copy = pltpu.make_async_copy(result, out_ref, result_sem.at[1])
    result_copy.start()
    for copy in all_copies:
        copy.wait_recv()
    keep.wait()
    result_copy.wait()

    for copy in mate_copies + all_copies:
        copy.wait_send()
    for copy in (field_copy, answer_copy, inner_copy, leaf_copy, outs_copy):
        copy.wait_send()
    for step in range(per_stage):
        block_copy(step).wait_send()


def shards(leaf_factor, class_maps, depth_class, owners, top_in):
    factor = leaf_factor[0, 0]
    leaves_here, leaf = factor.shape[0], factor.shape[1]
    half, quarter = leaves_here // 2, leaves_here // 4
    inside = leaf // 2
    columns = lax.axis_size("bx")
    most = max(2, (3 * leaves_here + 2 * columns - 1) // (2 * columns))
    whole = pl.BlockSpec(memory_space=pl.ANY)
    top_out, arrived = pl.pallas_call(
        functools.partial(kernel, columns, most),
        out_shape=(
            jax.ShapeDtypeStruct((quarter, 2 * leaf), F32),
            jax.ShapeDtypeStruct((columns, most, leaf), F32),
        ),
        in_specs=[whole] * 5,
        out_specs=(whole, whole),
        scratch_shapes=[
            pltpu.SMEM(depth_class.shape[1:], jnp.int32),
            pltpu.VMEM(class_maps.shape, BF16),
            pltpu.VMEM((1, leaves_here), jnp.int32),
            pltpu.VMEM((quarter, 2 * leaf), F32),
            pltpu.VMEM((2, half, leaf, leaf), BF16),
            pltpu.VMEM((2, half, leaf, leaf), F32),
            pltpu.VMEM((half, inside, 2 * leaf), F32),
            pltpu.VMEM((3, quarter // 2, inside, leaf), F32),
            pltpu.VMEM((3, quarter, 1, leaf), F32),
            pltpu.VMEM((2, 2, quarter, 1, leaf), F32),
            pltpu.VMEM((2, quarter, 1, leaf), F32),
            pltpu.VMEM((quarter, inside, inside), F32),
            pltpu.VMEM((quarter, inside, inside), F32),
            pltpu.VMEM((2, 2, quarter, 1, leaf), F32),
            pltpu.VMEM((2, quarter, 1, leaf), F32),
            pltpu.VMEM((2, half, leaf), F32),
            pltpu.VMEM((2, half, leaf), F32),
            pltpu.VMEM((columns, most, leaf), F32),
            pltpu.VMEM((2, quarter, leaf), F32),
            pltpu.VMEM((quarter, leaf), F32),
            pltpu.VMEM((quarter, 2 * leaf), F32),
            pltpu.SemaphoreType.DMA((4,)),
            pltpu.SemaphoreType.DMA((2,)),
            pltpu.SemaphoreType.DMA((half // GROUP,)),
            pltpu.SemaphoreType.DMA((half // GROUP,)),
            pltpu.SemaphoreType.DMA((half // GROUP,)),
            pltpu.SemaphoreType.DMA((2,)),
            pltpu.SemaphoreType.DMA((quarter // GROUP,)),
            pltpu.SemaphoreType.DMA((quarter // GROUP,)),
            pltpu.SemaphoreType.DMA((2,)),
            pltpu.SemaphoreType.DMA((2,)),
            pltpu.SemaphoreType.DMA((2,)),
            pltpu.SemaphoreType.DMA((2,)),
            pltpu.SemaphoreType.DMA((columns - 1,)),
            pltpu.SemaphoreType.DMA((columns - 1,)),
        ],
        compiler_params=pltpu.CompilerParams(
            collective_id=0, has_side_effects=True, vmem_limit_bytes=40 * 1024 * 1024
        ),
    )(depth_class[0], factor, class_maps, owners[0, 0].reshape(1, leaves_here), top_in[0, 0])
    return (top_out[None, None], arrived[None, None])


def solution(mesh):
    placed = (
        P("bx", "by", "seastate", None, None),
        P("seastate", None, None),
        P("bx", None, "seastate"),
        P("bx", "by", "seastate", None),
        P("bx", "by", "seastate", None),
    )
    return jax.shard_map(
        shards,
        mesh=mesh,
        in_specs=placed,
        out_specs=(P("bx", "by", "seastate", None), P("bx", "by", None, "seastate", None)),
        check_vma=False,
    )
```

```python
import functools

import jax
import jax.numpy as jnp
from jax import lax
from jax.experimental import pallas as pl
from jax.experimental.pallas import tpu as pltpu
from jax.sharding import PartitionSpec as P

MESH = pl.DeviceIdType.MESH
F32 = jnp.float32
BF16 = jnp.bfloat16
GROUP = 8
LEVELS = 32767.0


def halves(value):
    high = value.astype(BF16)
    return high, (value - high.astype(F32)).astype(BF16)


def product(left, right):
    left_high, left_low = halves(left)
    right_high, right_low = halves(right)
    return jnp.dot(
        jnp.concatenate([left_high, left_high, left_low], axis=1),
        jnp.concatenate([right_high, right_low, right_high], axis=0),
        preferred_element_type=F32,
    )


def lane_sums(values):
    ones = jnp.ones((2 * values.shape[1], values.shape[1]), BF16)
    return jnp.dot(
        jnp.concatenate(halves(values), axis=1), ones, preferred_element_type=F32
    )


def kernel(
    columns,
    most,
    classes_hbm,
    factor_ref,
    maps_hbm,
    owners_hbm,
    top_hbm,
    out_ref,
    delivered_ref,
    classes_ref,
    maps_ref,
    owners_ref,
    top_ref,
    factors,
    leaf_maps,
    inward,
    levels,
    blocks,
    coded,
    coded_in,
    answers,
    fields,
    fields_out,
    transposed,
    opened,
    inner,
    inner_out,
    leaves,
    home,
    outgoing,
    outs,
    outs_out,
    result,
    operand_sem,
    result_sem,
    local_sem,
    factor_send,
    factor_recv,
    field_sem,
    block_send,
    block_recv,
    answer_sem,
    inner_sem,
    leaf_sem,
    outs_sem,
    all_send,
    all_recv,
):
    leaves_here, leaf = factor_ref.shape[0], factor_ref.shape[1]
    face = leaf // 4
    half, quarter = leaves_here // 2, leaves_here // 4
    pairs = quarter // 2
    per_stage = quarter // GROUP
    turns = 2 * per_stage
    row, column = lax.axis_index("by"), lax.axis_index("bx")
    rp, cp = lax.rem(row, 2), lax.rem(column, 2)
    row_mate, column_mate = row + 1 - 2 * rp, column + 1 - 2 * cp
    first, second = (1 - cp) * quarter, cp * quarter
    west = cp == 0

    def to_row_mate(source, target, send, recv):
        return pltpu.make_async_remote_copy(
            src_ref=source, dst_ref=target, send_sem=send, recv_sem=recv,
            device_id={"by": row_mate}, device_id_type=MESH,
        )

    def to_column_mate(source, target, send, recv):
        return pltpu.make_async_remote_copy(
            src_ref=source, dst_ref=target, send_sem=send, recv_sem=recv,
            device_id={"bx": column_mate}, device_id_type=MESH,
        )

    operands = [
        pltpu.make_async_copy(source, target, operand_sem.at[index])
        for index, (source, target) in enumerate(
            (
                (top_hbm, top_ref),
                (classes_hbm, classes_ref),
                (maps_hbm, maps_ref),
                (owners_hbm, owners_ref),
            )
        )
    ]
    for copy in operands:
        copy.start()
    own_copies, mate_copies = [], []
    begins = [start + GROUP * index for start in (first, second) for index in range(per_stage)]
    for index, begin in enumerate(begins):
        own = pltpu.make_async_copy(
            factor_ref.at[pl.ds(rp * half + begin, GROUP)],
            factors.at[rp, pl.ds(begin, GROUP)],
            local_sem.at[index],
        )
        own.start()
        own_copies.append(own)
        mate_copies.append(
            to_row_mate(
                factor_ref.at[pl.ds((1 - rp) * half + begin, GROUP)],
                factors.at[rp, pl.ds(begin, GROUP)],
                factor_send.at[index],
                factor_recv.at[index],
            )
        )

    barrier = pltpu.get_barrier_semaphore()
    pl.semaphore_signal(barrier, inc=1, device_id={"by": row_mate}, device_id_type=MESH)
    for step in range(1, columns):
        pl.semaphore_signal(
            barrier, inc=1, device_id={"bx": lax.rem(column + step, columns)}, device_id_type=MESH
        )
    pl.semaphore_wait(barrier, columns)
    for copy in mate_copies:
        copy.start()

    operands[0].wait()
    top = top_ref[...]
    none = jnp.zeros((quarter, face), F32)

    def part(index):
        return top[:, index * face : (index + 1) * face]

    def row_of(*parts):
        return jnp.concatenate(parts, axis=1)

    sides = (
        (row_of(part(0), none, part(4), none), row_of(part(1), none, none, part(6))),
        (row_of(none, part(2), part(5), none), row_of(none, part(3), none, part(7))),
    )
    for index in range(2):
        mine = jnp.where(west, sides[0][index], sides[1][index])
        other = jnp.where(west, sides[1][index], sides[0][index])
        for box in range(quarter):
            fields[cp, index, box] = mine[box : box + 1]
            fields_out[index, box] = other[box : box + 1]
    field_copy = to_column_mate(fields_out, fields.at[cp], field_sem.at[0], field_sem.at[1])
    field_copy.start()

    sub_face = lax.broadcasted_iota(jnp.int32, (face, face), 0)
    lane_face = lax.broadcasted_iota(jnp.int32, (face, face), 1)
    identity = (sub_face == lane_face).astype(F32)
    sub_two = lax.broadcasted_iota(jnp.int32, (2 * face, leaf), 0)
    lane_two = lax.broadcasted_iota(jnp.int32, (2 * face, leaf), 1)
    no_map = jnp.zeros((face, leaf), F32)

    def block_copy(step):
        return to_column_mate(
            coded.at[0, pl.ds(step * (GROUP // 2), GROUP // 2)],
            coded_in.at[pl.ds(step * (GROUP // 2), GROUP // 2)],
            block_send.at[step],
            block_recv.at[step],
        )

    def inner_rows(matrix):
        return jnp.where(west, matrix[face : 2 * face], matrix[:face])

    picker_row = lax.broadcasted_iota(jnp.int32, (8 * leaf, leaf), 0)
    picker_lane = lax.broadcasted_iota(jnp.int32, (8 * leaf, leaf), 1)
    piece, source = picker_row // leaf, lax.rem(picker_row, leaf) - face * (1 - cp)
    spot = 2 * face * (piece // 4) + face * (lax.rem(piece, 2)) + source
    picker = jnp.where((source >= 0) & (source < face) & (picker_lane == spot), 1.0, 0.0).astype(BF16)

    def upward(turn, carry):
        stage, step = turn // per_stage, lax.rem(turn, per_stage)
        side = jnp.where(stage == 0, 1 - cp, cp)
        slot = jnp.where(stage == 0, 0, 1 + cp)
        for index in range(turns):

            @pl.when(turn == index)
            def _():
                own_copies[index].wait()
                mate_copies[index].wait_recv()

        boxes = [step * GROUP + index for index in range(GROUP)]
        places = [side * quarter + box for box in boxes]
        maps_a, maps_b = [], []
        for place in places:
            class_a = classes_ref[row - rp, rp * half + place]
            class_b = classes_ref[row - rp + 1, rp * half + place]
            map_a = jnp.dot(maps_ref[class_a], factors[0, place], preferred_element_type=F32)
            map_b = jnp.dot(maps_ref[class_b], factors[1, place], preferred_element_type=F32)
            leaf_maps[0, place] = map_a
            leaf_maps[1, place] = map_b
            maps_a.append(map_a)
            maps_b.append(map_b)
        rows_a = [m[3 * face :] for m in maps_a]
        rows_b = [m[2 * face : 3 * face] for m in maps_b]
        inner_a = [inner_rows(m) for m in maps_a]
        inner_b = [inner_rows(m) for m in maps_b]
        firsts = [
            product(jnp.concatenate([b, i], axis=0)[:, 2 * face : 3 * face], a)
            for b, i, a in zip(rows_b, inner_b, rows_a)
        ]
        starts = [jnp.concatenate([f[:face], -b], axis=1) for f, b in zip(firsts, rows_b)]
        lefts = [
            jnp.concatenate([f[:face], a, i, f[face:]], axis=0)[:, 3 * face :]
            for f, a, i in zip(firsts, rows_a, inner_a)
        ]
        seconds = [product(left, left[:face]) for left in lefts]
        rights = [st + product(sec[:face], st) for st, sec in zip(starts, seconds)]
        spreads = [
            product(
                jnp.concatenate([identity + left[:face], left[face:] + sec[face:]], axis=0), right
            )
            for left, sec, right in zip(lefts, seconds, rights)
        ]
        inward_a = [sp[:face] for sp in spreads]
        inward_b = [
            -jnp.concatenate([a, no_map], axis=1) - sp[face : 2 * face]
            for a, sp in zip(rows_a, spreads)
        ]
        upper = [
            jnp.concatenate([i, no_map], axis=1) + sp[2 * face : 3 * face]
            for i, sp in zip(inner_a, spreads)
        ]
        lower = [
            jnp.concatenate([-f[face:], i], axis=1) - sp[3 * face :]
            for f, i, sp in zip(firsts, inner_b, spreads)
        ]
        pieces = []
        for index, place in enumerate(places):
            inward[place, :face] = inward_a[index]
            inward[place, face:] = inward_b[index]
            level = jnp.concatenate([upper[index], lower[index]], axis=0)
            levels[place] = level
            pieces.append(jnp.concatenate(halves(level), axis=1))
        packed = jnp.dot(
            jnp.concatenate(
                [
                    jnp.concatenate([pieces[index], pieces[index + 1]], axis=1)
                    for index in range(0, GROUP, 2)
                ],
                axis=0,
            ),
            picker,
            preferred_element_type=F32,
        )
        for index in range(GROUP // 2):
            tile = packed[index * 2 * face : (index + 1) * 2 * face]
            pair = step * (GROUP // 2) + index
            blocks[stage, pair] = tile
            scale = jnp.maximum(jnp.max(jnp.abs(tile), axis=0, keepdims=True), 1e-30)
            code = jnp.round(tile * (LEVELS / scale))
            coded[stage, pair] = code.astype(jnp.int32).astype(jnp.int16)
            answers[slot, quarter + pair] = scale * (1.0 / LEVELS)

        @pl.when(stage == 0)
        def _():
            block_copy(step).start()

        return carry

    operands[1].wait()
    operands[2].wait()
    lax.fori_loop(0, turns, upward, 0)

    def answer(turn, carry):
        stage, step = turn // per_stage, lax.rem(turn, per_stage)
        side = jnp.where(stage == 0, 1 - cp, cp)
        slot = jnp.where(stage == 0, 0, 1 + cp)
        parts = []
        for index in range(GROUP):
            box = step * GROUP + index
            level = levels[side * quarter + box]
            parts.append(
                level[:, :leaf] * fields[side, 0, box] + level[:, leaf:] * fields[side, 1, box]
            )
        sums = lane_sums(jnp.concatenate(parts, axis=0))
        for index in range(GROUP):
            answers[slot, step * GROUP + index] = jnp.sum(
                jnp.where(
                    sub_two == lane_two, sums[index * 2 * face : (index + 1) * 2 * face], 0.0
                ),
                axis=0,
                keepdims=True,
            )
        return carry

    field_copy.wait_recv()
    lax.fori_loop(0, per_stage, answer, 0)
    answer_copy = to_column_mate(
        answers.at[0], answers.at[1 + cp], answer_sem.at[0], answer_sem.at[1]
    )
    answer_copy.start()
    lax.fori_loop(per_stage, turns, answer, 0)

    operands[3].wait()
    target = owners_ref[...]
    named = (lax.broadcasted_iota(jnp.int32, (columns, leaves_here), 0) == target).astype(F32)
    before = lax.broadcasted_iota(jnp.int32, (leaves_here, leaves_here), 0) < (
        lax.broadcasted_iota(jnp.int32, (leaves_here, leaves_here), 1)
    )
    earlier = jnp.dot(
        named.astype(BF16), before.astype(F32).astype(BF16), preferred_element_type=F32
    )
    rank = jnp.sum(named * earlier, axis=0, keepdims=True)
    slots = target.astype(F32) * most + rank
    wanted = lax.broadcasted_iota(jnp.int32, (columns * most, leaves_here), 0).astype(F32)
    selector = (wanted == slots).astype(F32).astype(BF16)

    for step in range(per_stage):
        block_copy(step).wait_recv()
    answer_copy.wait_recv()
    for index in range(pairs):
        mine = blocks[1, index]
        received = coded_in[index].astype(jnp.int32).astype(F32)
        received = received * answers[2 - cp, quarter + index]
        both = jnp.where(west, mine, received).T
        transposed[2 * index] = both[: 2 * face]
        transposed[2 * index + 1] = both[2 * face :]
        other = jnp.where(west, received, mine)
        opened[2 * index] = other[:, : 2 * face]
        opened[2 * index + 1] = other[:, 2 * face :]
    diagonal = (
        lax.broadcasted_iota(jnp.int32, (quarter, 2 * face, 2 * face), 1)
        == lax.broadcasted_iota(jnp.int32, (quarter, 2 * face, 2 * face), 2)
    )
    west_out = answers[1][:quarter, :, : 2 * face]
    east_out = answers[2][:quarter, :, : 2 * face]
    start = jnp.sum(
        opened[...] * west_out - jnp.where(diagonal, east_out, 0.0), axis=2, keepdims=True
    )
    value = start
    for _ in range(3):
        between = jnp.sum(transposed[...] * value, axis=1, keepdims=True)
        value = start + jnp.sum(opened[...] * between, axis=2, keepdims=True)
    to_west = jnp.sum(jnp.where(diagonal, value, 0.0), axis=1, keepdims=True)
    to_east = -west_out - jnp.sum(transposed[...] * value, axis=1, keepdims=True)
    gap = jnp.zeros((quarter, 1, face), F32)
    gaps = jnp.zeros((quarter, 1, 2 * face), F32)
    west_rows = (
        jnp.concatenate([gap, to_west[:, :, :face], gaps], axis=2),
        jnp.concatenate([gap, to_west[:, :, face:], gaps], axis=2),
    )
    east_rows = (
        jnp.concatenate([to_east[:, :, :face], gap, gaps], axis=2),
        jnp.concatenate([to_east[:, :, face:], gap, gaps], axis=2),
    )
    for index in range(2):
        inner[cp, index] = jnp.where(west, west_rows[index], east_rows[index])
        inner_out[index] = jnp.where(west, east_rows[index], west_rows[index])
    inner_copy = to_column_mate(inner_out, inner.at[cp], inner_sem.at[0], inner_sem.at[1])
    inner_copy.start()

    sub_row = lax.broadcasted_iota(jnp.int32, (face, leaf), 0)
    lane_row = lax.broadcasted_iota(jnp.int32, (face, leaf), 1)

    def downward(turn, carry):
        stage, step = turn // per_stage, lax.rem(turn, per_stage)
        side = jnp.where(stage == 0, cp, 1 - cp)
        parts, known = [], []
        for index in range(GROUP):
            box = step * GROUP + index
            field_a = fields[side, 0, box] + inner[side, 0, box]
            field_b = fields[side, 1, box] + inner[side, 1, box]
            both = inward[side * quarter + box]
            parts.append(both[:, :leaf] * field_a + both[:, leaf:] * field_b)
            known.append((field_a, field_b))
        sums = lane_sums(jnp.concatenate(parts, axis=0))
        for index in range(GROUP):
            place = side * quarter + step * GROUP + index
            found = sums[index * 2 * face : (index + 1) * 2 * face]
            north = jnp.where(lane_row == sub_row + 3 * face, found[:face], 0.0)
            south = jnp.where(lane_row == sub_row + 2 * face, found[face:], 0.0)
            leaves[0, pl.ds(place, 1)] = known[index][0] + jnp.sum(north, axis=0, keepdims=True)
            leaves[1, pl.ds(place, 1)] = known[index][1] + jnp.sum(south, axis=0, keepdims=True)
        return carry

    lax.fori_loop(0, per_stage, downward, 0)
    inner_copy.wait_recv()
    lax.fori_loop(per_stage, turns, downward, 0)
    leaf_copy = to_row_mate(leaves.at[1 - rp], home.at[rp], leaf_sem.at[0], leaf_sem.at[1])
    leaf_copy.start()
    home[rp] = leaves[rp]

    sub_all = lax.broadcasted_iota(jnp.int32, (leaf, leaf), 0)
    lane_all = lax.broadcasted_iota(jnp.int32, (leaf, leaf), 1)

    def outward(side, target_ref):
        def body(turn, carry):
            parts = []
            for index in range(GROUP):
                place = side * quarter + turn * GROUP + index
                leaf_a = leaves[0, pl.ds(place, 1)]
                leaf_b = leaves[1, pl.ds(place, 1)]
                outer = pl.ds(cp * face, face)
                parts += [
                    leaf_maps[0, place, outer] * leaf_a,
                    leaf_maps[1, place, outer] * leaf_b,
                    leaf_maps[0, place, 2 * face : 3 * face] * leaf_a,
                    leaf_maps[1, place, 3 * face :] * leaf_b,
                ]
            sums = lane_sums(jnp.concatenate(parts, axis=0))
            for index in range(GROUP):
                target_ref[pl.ds(turn * GROUP + index, 1)] = jnp.sum(
                    jnp.where(
                        sub_all == lane_all, sums[index * leaf : (index + 1) * leaf], 0.0
                    ),
                    axis=0,
                    keepdims=True,
                )
            return carry

        lax.fori_loop(0, per_stage, body, 0)

    outward(1 - cp, outs_out)
    outs_copy = to_column_mate(outs_out, outs.at[cp], outs_sem.at[0], outs_sem.at[1])
    outs_copy.start()

    leaf_copy.wait_recv()
    values = jnp.concatenate([home[0], home[1]], axis=0)
    high, rest = halves(values)
    middle, low = halves(values - high.astype(F32))
    chosen = (
        jnp.dot(selector, high, preferred_element_type=F32)
        + jnp.dot(selector, middle, preferred_element_type=F32)
        + jnp.dot(selector, low, preferred_element_type=F32)
    )
    for owner in range(columns):
        outgoing[owner] = chosen[owner * most : (owner + 1) * most]
    all_copies = []
    for step in range(1, columns):
        owner = lax.rem(column + step, columns)
        copy = pltpu.make_async_remote_copy(
            src_ref=outgoing.at[owner],
            dst_ref=delivered_ref.at[column],
            send_sem=all_send.at[step - 1],
            recv_sem=all_recv.at[step - 1],
            device_id={"bx": owner},
            device_id_type=MESH,
        )
        copy.start()
        all_copies.append(copy)
    keep = pltpu.make_async_copy(
        outgoing.at[column], delivered_ref.at[column], result_sem.at[0]
    )
    keep.start()

    outward(cp, outs.at[cp])
    outs_copy.wait_recv()
    out_west, out_east = outs[0], outs[1]
    result[...] = jnp.concatenate(
        [
            out_west[:, : 2 * face],
            out_east[:, : 2 * face],
            out_west[:, 2 * face : 3 * face],
            out_east[:, 2 * face : 3 * face],
            out_west[:, 3 * face :],
            out_east[:, 3 * face :],
        ],
        axis=1,
    )
    result_copy = pltpu.make_async_copy(result, out_ref, result_sem.at[1])
    result_copy.start()
    for copy in all_copies:
        copy.wait_recv()
    keep.wait()
    result_copy.wait()

    for copy in mate_copies + all_copies:
        copy.wait_send()
    for copy in (field_copy, answer_copy, inner_copy, leaf_copy, outs_copy):
        copy.wait_send()
    for step in range(per_stage):
        block_copy(step).wait_send()


def shards(leaf_factor, class_maps, depth_class, owners, top_in):
    factor = leaf_factor[0, 0]
    leaves_here, leaf = factor.shape[0], factor.shape[1]
    half, quarter = leaves_here // 2, leaves_here // 4
    inside = leaf // 2
    columns = lax.axis_size("bx")
    most = max(2, (3 * leaves_here + 2 * columns - 1) // (2 * columns))
    whole = pl.BlockSpec(memory_space=pl.ANY)
    top_out, arrived = pl.pallas_call(
        functools.partial(kernel, columns, most),
        out_shape=(
            jax.ShapeDtypeStruct((quarter, 2 * leaf), F32),
            jax.ShapeDtypeStruct((columns, most, leaf), F32),
        ),
        in_specs=[whole] * 5,
        out_specs=(whole, whole),
        scratch_shapes=[
            pltpu.SMEM(depth_class.shape[1:], jnp.int32),
            pltpu.VMEM(class_maps.shape, BF16),
            pltpu.VMEM((1, leaves_here), jnp.int32),
            pltpu.VMEM((quarter, 2 * leaf), F32),
            pltpu.VMEM((2, half, leaf, leaf), BF16),
            pltpu.VMEM((2, half, leaf, leaf), F32),
            pltpu.VMEM((half, inside, 2 * leaf), F32),
            pltpu.VMEM((half, inside, 2 * leaf), F32),
            pltpu.VMEM((2, quarter // 2, inside, leaf), F32),
            pltpu.VMEM((2, quarter // 2, inside, leaf), jnp.int16),
            pltpu.VMEM((quarter // 2, inside, leaf), jnp.int16),
            pltpu.VMEM((3, quarter + quarter // 2, 1, leaf), F32),
            pltpu.VMEM((2, 2, quarter, 1, leaf), F32),
            pltpu.VMEM((2, quarter, 1, leaf), F32),
            pltpu.VMEM((quarter, inside, inside), F32),
            pltpu.VMEM((quarter, inside, inside), F32),
            pltpu.VMEM((2, 2, quarter, 1, leaf), F32),
            pltpu.VMEM((2, quarter, 1, leaf), F32),
            pltpu.VMEM((2, half, leaf), F32),
            pltpu.VMEM((2, half, leaf), F32),
            pltpu.VMEM((columns, most, leaf), F32),
            pltpu.VMEM((2, quarter, leaf), F32),
            pltpu.VMEM((quarter, leaf), F32),
            pltpu.VMEM((quarter, 2 * leaf), F32),
            pltpu.SemaphoreType.DMA((4,)),
            pltpu.SemaphoreType.DMA((2,)),
            pltpu.SemaphoreType.DMA((half // GROUP,)),
            pltpu.SemaphoreType.DMA((half // GROUP,)),
            pltpu.SemaphoreType.DMA((half // GROUP,)),
            pltpu.SemaphoreType.DMA((2,)),
            pltpu.SemaphoreType.DMA((quarter // GROUP,)),
            pltpu.SemaphoreType.DMA((quarter // GROUP,)),
            pltpu.SemaphoreType.DMA((2,)),
            pltpu.SemaphoreType.DMA((2,)),
            pltpu.SemaphoreType.DMA((2,)),
            pltpu.SemaphoreType.DMA((2,)),
            pltpu.SemaphoreType.DMA((columns - 1,)),
            pltpu.SemaphoreType.DMA((columns - 1,)),
        ],
        compiler_params=pltpu.CompilerParams(
            collective_id=0, has_side_effects=True, vmem_limit_bytes=60 * 1024 * 1024
        ),
    )(depth_class[0], factor, class_maps, owners[0, 0].reshape(1, leaves_here), top_in[0, 0])
    return (top_out[None, None], arrived[None, None])


def solution(mesh):
    placed = (
        P("bx", "by", "seastate", None, None),
        P("seastate", None, None),
        P("bx", None, "seastate"),
        P("bx", "by", "seastate", None),
        P("bx", "by", "seastate", None),
    )
    return jax.shard_map(
        shards,
        mesh=mesh,
        in_specs=placed,
        out_specs=(P("bx", "by", "seastate", None), P("bx", "by", None, "seastate", None)),
        check_vma=False,
    )
```

```python
import functools

import jax
import jax.numpy as jnp
from jax import lax
from jax.experimental import pallas as pl
from jax.experimental.pallas import tpu as pltpu
from jax.sharding import PartitionSpec as P

MESH = pl.DeviceIdType.MESH
F32 = jnp.float32
BF16 = jnp.bfloat16
GROUP = 16
LEVELS = 32767.0


def halves(value):
    high = value.astype(BF16)
    return high, (value - high.astype(F32)).astype(BF16)


def product(left, right):
    left_high, left_low = halves(left)
    right_high, right_low = halves(right)
    return jnp.dot(
        jnp.concatenate([left_high, left_high, left_low], axis=1),
        jnp.concatenate([right_high, right_low, right_high], axis=0),
        preferred_element_type=F32,
    )


def lane_sums(values):
    ones = jnp.ones((2 * values.shape[1], values.shape[1]), BF16)
    return jnp.dot(
        jnp.concatenate(halves(values), axis=1), ones, preferred_element_type=F32
    )


def kernel(
    columns,
    most,
    classes_hbm,
    factor_ref,
    maps_hbm,
    owners_hbm,
    top_hbm,
    out_ref,
    delivered_ref,
    classes_ref,
    maps_ref,
    owners_ref,
    top_ref,
    factors,
    leaf_maps,
    inward,
    levels,
    blocks,
    coded,
    coded_in,
    answers,
    fields,
    fields_out,
    transposed,
    opened,
    inner,
    inner_out,
    leaves,
    home,
    outgoing,
    outs,
    outs_out,
    result,
    operand_sem,
    result_sem,
    local_sem,
    factor_send,
    factor_recv,
    field_sem,
    block_send,
    block_recv,
    answer_sem,
    inner_sem,
    leaf_sem,
    outs_sem,
    all_send,
    all_recv,
):
    leaves_here, leaf = factor_ref.shape[0], factor_ref.shape[1]
    face = leaf // 4
    half, quarter = leaves_here // 2, leaves_here // 4
    pairs = quarter // 2
    per_stage = quarter // GROUP
    turns = 2 * per_stage
    row, column = lax.axis_index("by"), lax.axis_index("bx")
    rp, cp = lax.rem(row, 2), lax.rem(column, 2)
    row_mate, column_mate = row + 1 - 2 * rp, column + 1 - 2 * cp
    first, second = (1 - cp) * quarter, cp * quarter
    west = cp == 0

    def to_row_mate(source, target, send, recv):
        return pltpu.make_async_remote_copy(
            src_ref=source, dst_ref=target, send_sem=send, recv_sem=recv,
            device_id={"by": row_mate}, device_id_type=MESH,
        )

    def to_column_mate(source, target, send, recv):
        return pltpu.make_async_remote_copy(
            src_ref=source, dst_ref=target, send_sem=send, recv_sem=recv,
            device_id={"bx": column_mate}, device_id_type=MESH,
        )

    operands = [
        pltpu.make_async_copy(source, target, operand_sem.at[index])
        for index, (source, target) in enumerate(
            (
                (top_hbm, top_ref),
                (classes_hbm, classes_ref),
                (maps_hbm, maps_ref),
                (owners_hbm, owners_ref),
            )
        )
    ]
    for copy in operands:
        copy.start()
    own_copies, mate_copies = [], []
    begins = [start + GROUP * index for start in (first, second) for index in range(per_stage)]
    for index, begin in enumerate(begins):
        own = pltpu.make_async_copy(
            factor_ref.at[pl.ds(rp * half + begin, GROUP)],
            factors.at[rp, pl.ds(begin, GROUP)],
            local_sem.at[index],
        )
        own.start()
        own_copies.append(own)
        mate_copies.append(
            to_row_mate(
                factor_ref.at[pl.ds((1 - rp) * half + begin, GROUP)],
                factors.at[rp, pl.ds(begin, GROUP)],
                factor_send.at[index],
                factor_recv.at[index],
            )
        )

    barrier = pltpu.get_barrier_semaphore()
    pl.semaphore_signal(barrier, inc=1, device_id={"by": row_mate}, device_id_type=MESH)
    for step in range(1, columns):
        pl.semaphore_signal(
            barrier, inc=1, device_id={"bx": lax.rem(column + step, columns)}, device_id_type=MESH
        )
    pl.semaphore_wait(barrier, columns)
    for copy in mate_copies:
        copy.start()

    operands[0].wait()
    top = top_ref[...]
    none = jnp.zeros((quarter, face), F32)

    def part(index):
        return top[:, index * face : (index + 1) * face]

    def row_of(*parts):
        return jnp.concatenate(parts, axis=1)

    sides = (
        (row_of(part(0), none, part(4), none), row_of(part(1), none, none, part(6))),
        (row_of(none, part(2), part(5), none), row_of(none, part(3), none, part(7))),
    )
    for index in range(2):
        mine = jnp.where(west, sides[0][index], sides[1][index])
        other = jnp.where(west, sides[1][index], sides[0][index])
        for box in range(quarter):
            fields[cp, index, box] = mine[box : box + 1]
            fields_out[index, box] = other[box : box + 1]
    field_copy = to_column_mate(fields_out, fields.at[cp], field_sem.at[0], field_sem.at[1])
    field_copy.start()

    sub_face = lax.broadcasted_iota(jnp.int32, (face, face), 0)
    lane_face = lax.broadcasted_iota(jnp.int32, (face, face), 1)
    identity = (sub_face == lane_face).astype(F32)
    sub_two = lax.broadcasted_iota(jnp.int32, (2 * face, leaf), 0)
    lane_two = lax.broadcasted_iota(jnp.int32, (2 * face, leaf), 1)
    no_map = jnp.zeros((face, leaf), F32)

    def block_copy(step):
        return to_column_mate(
            coded.at[0, pl.ds(step * (GROUP // 2), GROUP // 2)],
            coded_in.at[pl.ds(step * (GROUP // 2), GROUP // 2)],
            block_send.at[step],
            block_recv.at[step],
        )

    def inner_rows(matrix):
        return jnp.where(west, matrix[face : 2 * face], matrix[:face])

    picker_row = lax.broadcasted_iota(jnp.int32, (8 * leaf, leaf), 0)
    picker_lane = lax.broadcasted_iota(jnp.int32, (8 * leaf, leaf), 1)
    piece, source = picker_row // leaf, lax.rem(picker_row, leaf) - face * (1 - cp)
    spot = 2 * face * (piece // 4) + face * (lax.rem(piece, 2)) + source
    picker = jnp.where((source >= 0) & (source < face) & (picker_lane == spot), 1.0, 0.0).astype(BF16)

    def upward(turn, carry):
        stage, step = turn // per_stage, lax.rem(turn, per_stage)
        side = jnp.where(stage == 0, 1 - cp, cp)
        slot = jnp.where(stage == 0, 0, 1 + cp)
        for index in range(turns):

            @pl.when(turn == index)
            def _():
                own_copies[index].wait()
                mate_copies[index].wait_recv()

        boxes = [step * GROUP + index for index in range(GROUP)]
        places = [side * quarter + box for box in boxes]
        maps_a, maps_b = [], []
        for place in places:
            class_a = classes_ref[row - rp, rp * half + place]
            class_b = classes_ref[row - rp + 1, rp * half + place]
            map_a = jnp.dot(maps_ref[class_a], factors[0, place], preferred_element_type=F32)
            map_b = jnp.dot(maps_ref[class_b], factors[1, place], preferred_element_type=F32)
            leaf_maps[0, place] = map_a
            leaf_maps[1, place] = map_b
            maps_a.append(map_a)
            maps_b.append(map_b)
        rows_a = [m[3 * face :] for m in maps_a]
        rows_b = [m[2 * face : 3 * face] for m in maps_b]
        inner_a = [inner_rows(m) for m in maps_a]
        inner_b = [inner_rows(m) for m in maps_b]
        firsts = [
            product(jnp.concatenate([b, i], axis=0)[:, 2 * face : 3 * face], a)
            for b, i, a in zip(rows_b, inner_b, rows_a)
        ]
        starts = [jnp.concatenate([f[:face], -b], axis=1) for f, b in zip(firsts, rows_b)]
        lefts = [
            jnp.concatenate([f[:face], a, i, f[face:]], axis=0)[:, 3 * face :]
            for f, a, i in zip(firsts, rows_a, inner_a)
        ]
        seconds = [product(left, left[:face]) for left in lefts]
        rights = [st + product(sec[:face], st) for st, sec in zip(starts, seconds)]
        spreads = [
            product(
                jnp.concatenate([identity + left[:face], left[face:] + sec[face:]], axis=0), right
            )
            for left, sec, right in zip(lefts, seconds, rights)
        ]
        inward_a = [sp[:face] for sp in spreads]
        inward_b = [
            -jnp.concatenate([a, no_map], axis=1) - sp[face : 2 * face]
            for a, sp in zip(rows_a, spreads)
        ]
        upper = [
            jnp.concatenate([i, no_map], axis=1) + sp[2 * face : 3 * face]
            for i, sp in zip(inner_a, spreads)
        ]
        lower = [
            jnp.concatenate([-f[face:], i], axis=1) - sp[3 * face :]
            for f, i, sp in zip(firsts, inner_b, spreads)
        ]
        pieces = []
        for index, place in enumerate(places):
            inward[place, :face] = inward_a[index]
            inward[place, face:] = inward_b[index]
            level = jnp.concatenate([upper[index], lower[index]], axis=0)
            levels[place] = level
            pieces.append(jnp.concatenate(halves(level), axis=1))
        packed = jnp.dot(
            jnp.concatenate(
                [
                    jnp.concatenate([pieces[index], pieces[index + 1]], axis=1)
                    for index in range(0, GROUP, 2)
                ],
                axis=0,
            ),
            picker,
            preferred_element_type=F32,
        )
        for index in range(GROUP // 2):
            tile = packed[index * 2 * face : (index + 1) * 2 * face]
            pair = step * (GROUP // 2) + index
            blocks[stage, pair] = tile
            scale = jnp.maximum(jnp.max(jnp.abs(tile), axis=0, keepdims=True), 1e-30)
            code = jnp.round(tile * (LEVELS / scale))
            coded[stage, pair] = code.astype(jnp.int32).astype(jnp.int16)
            answers[slot, quarter + pair] = scale * (1.0 / LEVELS)

        @pl.when(stage == 0)
        def _():
            block_copy(step).start()

        return carry

    operands[1].wait()
    operands[2].wait()
    lax.fori_loop(0, turns, upward, 0)

    def answer(turn, carry):
        stage, step = turn // per_stage, lax.rem(turn, per_stage)
        side = jnp.where(stage == 0, 1 - cp, cp)
        slot = jnp.where(stage == 0, 0, 1 + cp)
        parts = []
        for index in range(GROUP):
            box = step * GROUP + index
            level = levels[side * quarter + box]
            parts.append(
                level[:, :leaf] * fields[side, 0, box] + level[:, leaf:] * fields[side, 1, box]
            )
        sums = lane_sums(jnp.concatenate(parts, axis=0))
        for index in range(GROUP):
            answers[slot, step * GROUP + index] = jnp.sum(
                jnp.where(
                    sub_two == lane_two, sums[index * 2 * face : (index + 1) * 2 * face], 0.0
                ),
                axis=0,
                keepdims=True,
            )
        return carry

    field_copy.wait_recv()
    lax.fori_loop(0, per_stage, answer, 0)
    answer_copy = to_column_mate(
        answers.at[0], answers.at[1 + cp], answer_sem.at[0], answer_sem.at[1]
    )
    answer_copy.start()
    lax.fori_loop(per_stage, turns, answer, 0)

    operands[3].wait()
    target = owners_ref[...]
    named = (lax.broadcasted_iota(jnp.int32, (columns, leaves_here), 0) == target).astype(F32)
    before = lax.broadcasted_iota(jnp.int32, (leaves_here, leaves_here), 0) < (
        lax.broadcasted_iota(jnp.int32, (leaves_here, leaves_here), 1)
    )
    earlier = jnp.dot(
        named.astype(BF16), before.astype(F32).astype(BF16), preferred_element_type=F32
    )
    rank = jnp.sum(named * earlier, axis=0, keepdims=True)
    slots = target.astype(F32) * most + rank
    wanted = lax.broadcasted_iota(jnp.int32, (columns * most, leaves_here), 0).astype(F32)
    selector = (wanted == slots).astype(F32).astype(BF16)

    for step in range(per_stage):
        block_copy(step).wait_recv()
    answer_copy.wait_recv()
    for index in range(pairs):
        mine = blocks[1, index]
        received = coded_in[index].astype(jnp.int32).astype(F32)
        received = received * answers[2 - cp, quarter + index]
        both = jnp.where(west, mine, received).T
        transposed[2 * index] = both[: 2 * face]
        transposed[2 * index + 1] = both[2 * face :]
        other = jnp.where(west, received, mine)
        opened[2 * index] = other[:, : 2 * face]
        opened[2 * index + 1] = other[:, 2 * face :]
    diagonal = (
        lax.broadcasted_iota(jnp.int32, (quarter, 2 * face, 2 * face), 1)
        == lax.broadcasted_iota(jnp.int32, (quarter, 2 * face, 2 * face), 2)
    )
    west_out = answers[1][:quarter, :, : 2 * face]
    east_out = answers[2][:quarter, :, : 2 * face]
    start = jnp.sum(
        opened[...] * west_out - jnp.where(diagonal, east_out, 0.0), axis=2, keepdims=True
    )
    value = start
    for _ in range(3):
        between = jnp.sum(transposed[...] * value, axis=1, keepdims=True)
        value = start + jnp.sum(opened[...] * between, axis=2, keepdims=True)
    to_west = jnp.sum(jnp.where(diagonal, value, 0.0), axis=1, keepdims=True)
    to_east = -west_out - jnp.sum(transposed[...] * value, axis=1, keepdims=True)
    gap = jnp.zeros((quarter, 1, face), F32)
    gaps = jnp.zeros((quarter, 1, 2 * face), F32)
    west_rows = (
        jnp.concatenate([gap, to_west[:, :, :face], gaps], axis=2),
        jnp.concatenate([gap, to_west[:, :, face:], gaps], axis=2),
    )
    east_rows = (
        jnp.concatenate([to_east[:, :, :face], gap, gaps], axis=2),
        jnp.concatenate([to_east[:, :, face:], gap, gaps], axis=2),
    )
    for index in range(2):
        inner[cp, index] = jnp.where(west, west_rows[index], east_rows[index])
        inner_out[index] = jnp.where(west, east_rows[index], west_rows[index])
    inner_copy = to_column_mate(inner_out, inner.at[cp], inner_sem.at[0], inner_sem.at[1])
    inner_copy.start()

    sub_row = lax.broadcasted_iota(jnp.int32, (face, leaf), 0)
    lane_row = lax.broadcasted_iota(jnp.int32, (face, leaf), 1)

    def downward(turn, carry):
        stage, step = turn // per_stage, lax.rem(turn, per_stage)
        side = jnp.where(stage == 0, cp, 1 - cp)
        parts, known = [], []
        for index in range(GROUP):
            box = step * GROUP + index
            field_a = fields[side, 0, box] + inner[side, 0, box]
            field_b = fields[side, 1, box] + inner[side, 1, box]
            both = inward[side * quarter + box]
            parts.append(both[:, :leaf] * field_a + both[:, leaf:] * field_b)
            known.append((field_a, field_b))
        sums = lane_sums(jnp.concatenate(parts, axis=0))
        for index in range(GROUP):
            place = side * quarter + step * GROUP + index
            found = sums[index * 2 * face : (index + 1) * 2 * face]
            north = jnp.where(lane_row == sub_row + 3 * face, found[:face], 0.0)
            south = jnp.where(lane_row == sub_row + 2 * face, found[face:], 0.0)
            leaves[0, pl.ds(place, 1)] = known[index][0] + jnp.sum(north, axis=0, keepdims=True)
            leaves[1, pl.ds(place, 1)] = known[index][1] + jnp.sum(south, axis=0, keepdims=True)
        return carry

    lax.fori_loop(0, per_stage, downward, 0)
    inner_copy.wait_recv()
    lax.fori_loop(per_stage, turns, downward, 0)
    leaf_copy = to_row_mate(leaves.at[1 - rp], home.at[rp], leaf_sem.at[0], leaf_sem.at[1])
    leaf_copy.start()
    home[rp] = leaves[rp]

    sub_all = lax.broadcasted_iota(jnp.int32, (leaf, leaf), 0)
    lane_all = lax.broadcasted_iota(jnp.int32, (leaf, leaf), 1)

    def outward(side, target_ref):
        def body(turn, carry):
            parts = []
            for index in range(GROUP):
                place = side * quarter + turn * GROUP + index
                leaf_a = leaves[0, pl.ds(place, 1)]
                leaf_b = leaves[1, pl.ds(place, 1)]
                outer = pl.ds(cp * face, face)
                parts += [
                    leaf_maps[0, place, outer] * leaf_a,
                    leaf_maps[1, place, outer] * leaf_b,
                    leaf_maps[0, place, 2 * face : 3 * face] * leaf_a,
                    leaf_maps[1, place, 3 * face :] * leaf_b,
                ]
            sums = lane_sums(jnp.concatenate(parts, axis=0))
            for index in range(GROUP):
                target_ref[pl.ds(turn * GROUP + index, 1)] = jnp.sum(
                    jnp.where(
                        sub_all == lane_all, sums[index * leaf : (index + 1) * leaf], 0.0
                    ),
                    axis=0,
                    keepdims=True,
                )
            return carry

        lax.fori_loop(0, per_stage, body, 0)

    outward(1 - cp, outs_out)
    outs_copy = to_column_mate(outs_out, outs.at[cp], outs_sem.at[0], outs_sem.at[1])
    outs_copy.start()

    leaf_copy.wait_recv()
    values = jnp.concatenate([home[0], home[1]], axis=0)
    high, rest = halves(values)
    middle, low = halves(values - high.astype(F32))
    chosen = (
        jnp.dot(selector, high, preferred_element_type=F32)
        + jnp.dot(selector, middle, preferred_element_type=F32)
        + jnp.dot(selector, low, preferred_element_type=F32)
    )
    for owner in range(columns):
        outgoing[owner] = chosen[owner * most : (owner + 1) * most]
    all_copies = []
    for step in range(1, columns):
        owner = lax.rem(column + step, columns)
        copy = pltpu.make_async_remote_copy(
            src_ref=outgoing.at[owner],
            dst_ref=delivered_ref.at[column],
            send_sem=all_send.at[step - 1],
            recv_sem=all_recv.at[step - 1],
            device_id={"bx": owner},
            device_id_type=MESH,
        )
        copy.start()
        all_copies.append(copy)
    keep = pltpu.make_async_copy(
        outgoing.at[column], delivered_ref.at[column], result_sem.at[0]
    )
    keep.start()

    outward(cp, outs.at[cp])
    outs_copy.wait_recv()
    out_west, out_east = outs[0], outs[1]
    result[...] = jnp.concatenate(
        [
            out_west[:, : 2 * face],
            out_east[:, : 2 * face],
            out_west[:, 2 * face : 3 * face],
            out_east[:, 2 * face : 3 * face],
            out_west[:, 3 * face :],
            out_east[:, 3 * face :],
        ],
        axis=1,
    )
    result_copy = pltpu.make_async_copy(result, out_ref, result_sem.at[1])
    result_copy.start()
    for copy in all_copies:
        copy.wait_recv()
    keep.wait()
    result_copy.wait()

    for copy in mate_copies + all_copies:
        copy.wait_send()
    for copy in (field_copy, answer_copy, inner_copy, leaf_copy, outs_copy):
        copy.wait_send()
    for step in range(per_stage):
        block_copy(step).wait_send()


def relay(top_ref, rows_ref, out_ref, delivered_ref, sems):
    first = pltpu.make_async_copy(top_ref, out_ref, sems.at[0])
    second = pltpu.make_async_copy(rows_ref, delivered_ref, sems.at[1])
    first.start()
    second.start()
    first.wait()
    second.wait()


def shards(leaf_factor, class_maps, depth_class, owners, top_in):
    factor = leaf_factor[0, 0]
    leaves_here, leaf = factor.shape[0], factor.shape[1]
    half, quarter = leaves_here // 2, leaves_here // 4
    inside = leaf // 2
    columns = lax.axis_size("bx")
    most = max(2, (3 * leaves_here + 2 * columns - 1) // (2 * columns))
    whole = pl.BlockSpec(memory_space=pl.ANY)
    top_out, arrived = pl.pallas_call(
        functools.partial(kernel, columns, most),
        out_shape=(
            jax.ShapeDtypeStruct((quarter, 2 * leaf), F32),
            jax.ShapeDtypeStruct((columns, most, leaf), F32),
        ),
        in_specs=[whole] * 5,
        out_specs=(whole, whole),
        scratch_shapes=[
            pltpu.SMEM(depth_class.shape[1:], jnp.int32),
            pltpu.VMEM(class_maps.shape, BF16),
            pltpu.VMEM((1, leaves_here), jnp.int32),
            pltpu.VMEM((quarter, 2 * leaf), F32),
            pltpu.VMEM((2, half, leaf, leaf), BF16),
            pltpu.VMEM((2, half, leaf, leaf), F32),
            pltpu.VMEM((half, inside, 2 * leaf), F32),
            pltpu.VMEM((half, inside, 2 * leaf), F32),
            pltpu.VMEM((2, quarter // 2, inside, leaf), F32),
            pltpu.VMEM((2, quarter // 2, inside, leaf), jnp.int16),
            pltpu.VMEM((quarter // 2, inside, leaf), jnp.int16),
            pltpu.VMEM((3, quarter + quarter // 2, 1, leaf), F32),
            pltpu.VMEM((2, 2, quarter, 1, leaf), F32),
            pltpu.VMEM((2, quarter, 1, leaf), F32),
            pltpu.VMEM((quarter, inside, inside), F32),
            pltpu.VMEM((quarter, inside, inside), F32),
            pltpu.VMEM((2, 2, quarter, 1, leaf), F32),
            pltpu.VMEM((2, quarter, 1, leaf), F32),
            pltpu.VMEM((2, half, leaf), F32),
            pltpu.VMEM((2, half, leaf), F32),
            pltpu.VMEM((columns, most, leaf), F32),
            pltpu.VMEM((2, quarter, leaf), F32),
            pltpu.VMEM((quarter, leaf), F32),
            pltpu.VMEM((quarter, 2 * leaf), F32),
            pltpu.SemaphoreType.DMA((4,)),
            pltpu.SemaphoreType.DMA((2,)),
            pltpu.SemaphoreType.DMA((half // GROUP,)),
            pltpu.SemaphoreType.DMA((half // GROUP,)),
            pltpu.SemaphoreType.DMA((half // GROUP,)),
            pltpu.SemaphoreType.DMA((2,)),
            pltpu.SemaphoreType.DMA((quarter // GROUP,)),
            pltpu.SemaphoreType.DMA((quarter // GROUP,)),
            pltpu.SemaphoreType.DMA((2,)),
            pltpu.SemaphoreType.DMA((2,)),
            pltpu.SemaphoreType.DMA((2,)),
            pltpu.SemaphoreType.DMA((2,)),
            pltpu.SemaphoreType.DMA((columns - 1,)),
            pltpu.SemaphoreType.DMA((columns - 1,)),
        ],
        compiler_params=pltpu.CompilerParams(
            collective_id=0, has_side_effects=True, vmem_limit_bytes=60 * 1024 * 1024
        ),
    )(depth_class[0], factor, class_maps, owners[0, 0].reshape(1, leaves_here), top_in[0, 0])
    near = pl.BlockSpec(memory_space=pltpu.VMEM)
    top_out, arrived = pl.pallas_call(
        relay,
        out_shape=(
            jax.ShapeDtypeStruct(top_out.shape, F32),
            jax.ShapeDtypeStruct(arrived.shape, F32),
        ),
        in_specs=[near, near],
        out_specs=(whole, whole),
        scratch_shapes=[pltpu.SemaphoreType.DMA((2,))],
    )(top_out, arrived)
    return (top_out[None, None], arrived[None, None])


def solution(mesh):
    placed = (
        P("bx", "by", "seastate", None, None),
        P("seastate", None, None),
        P("bx", None, "seastate"),
        P("bx", "by", "seastate", None),
        P("bx", "by", "seastate", None),
    )
    return jax.shard_map(
        shards,
        mesh=mesh,
        in_specs=placed,
        out_specs=(P("bx", "by", "seastate", None), P("bx", "by", None, "seastate", None)),
        check_vma=False,
    )
```
